32 devices in a mesh: deme: 8 (over z, y), gen: 4 (over x, core).
Axes of the slice: x: 2, y: 2, z: 4, core: 2. Of those that a mesh axis runs over, the one named last changes fastest.
Arguments:
- freqs: float32 [2048, 128, 512], P('deme', 'gen'), may hold values from 0 to 1
- start_basis: float32 [512, 128], replicated, may hold values from -0.25 to 0.25
Outputs:
- core: float32 [2048, 128, 128], P('deme', 'gen')
- factor: float32 [512, 128], replicated
The draws below stay inside these ranges and needn't reach their ends.
All inputs are finite; a program needn't handle non-finite values.
Results may differ from the reference program's by a relative error of at most 0.0003.
Values sent between devices are 32-bit elements; how exact they have to be, the bound alone decides.
A program may use at most 64 MiB of HBM per device.

```python
import jax
import jax.numpy as jnp
from jax import lax

LOCI = 512
RANK = 128
ITERS = 4
DEMES = 2048
GENS = 128


def draw_freqs(key, part):
    key = jax.random.fold_in(key, 7)
    subkeys = jax.random.split(key, 9)
    factors = 16
    errors = jax.random.normal(subkeys[0], (DEMES, GENS, LOCI + 1), jnp.float32)
    roughness = jax.random.normal(subkeys[1], (factors, DEMES, GENS), jnp.float32)
    linkage = jax.random.uniform(subkeys[2], (LOCI,), jnp.float32, -0.7, 0.7)
    loading = jax.random.normal(subkeys[3], (factors, LOCI), jnp.float32)
    offset = jax.random.uniform(subkeys[4], (LOCI,), jnp.float32, -1.5, 1.5)
    locus_scale = jnp.exp(jax.random.uniform(subkeys[5], (LOCI,), jnp.float32, jnp.log(0.25), 0.0))
    wavenumber = jax.random.uniform(subkeys[6], (factors,), jnp.float32, 0.5, 3.0)
    phases = jax.random.uniform(subkeys[7], (factors,), jnp.float32, -jnp.pi, jnp.pi)
    drifts = jax.random.uniform(subkeys[8], (factors,), jnp.float32, -2.0, 2.0)
    position = (jnp.arange(DEMES, dtype=jnp.float32) + 0.5) / DEMES
    elapsed = (jnp.arange(GENS, dtype=jnp.float32) + 0.5) / GENS
    amplitude = 0.42 * jnp.power(0.85, jnp.arange(factors, dtype=jnp.float32))
    angle_part = 2.0 * jnp.pi * wavenumber[:, None, None] * position[None, :, None] + phases[:, None, None] + drifts[:, None, None] * elapsed[None, None, :]
    ancestry = amplitude[:, None, None] * (jnp.sin(angle_part) + 0.8 * roughness)
    logits = offset[None, None, :] + errors[:, :, 1:] + linkage[None, None, :] * errors[:, :, :-1]
    for index in range(factors):
        logits = logits + ancestry[index][:, :, None] * loading[index][None, None, :]
    return locus_scale[None, None, :] * jax.nn.sigmoid(logits)


def normal_values(own_key, dims, spread, limit, kind=jnp.bfloat16):
    values = jax.random.normal(own_key, dims, jnp.float32) * spread
    return jnp.minimum(jnp.maximum(values, -limit), limit).astype(kind)


def setup_inputs(seed: int = 0) -> dict:
    arg_keys = jax.random.split(jax.random.key(seed), 3)
    freqs = draw_freqs(jax.random.fold_in(arg_keys[2], 71), 0)
    start_basis = normal_values(arg_keys[1], (LOCI, RANK), LOCI ** -0.5, 0.25, jnp.float32)
    return {"freqs": freqs, "start_basis": start_basis}


def orthonormal(z):
    small = jnp.dot(z.T.astype(jnp.float32), z.astype(jnp.float32), precision=lax.Precision.HIGHEST, preferred_element_type=jnp.float32)
    lower = jnp.linalg.cholesky(small)
    return jax.scipy.linalg.solve_triangular(lower, z.T, lower=True).T

def reference(freqs, start_basis):
    mean = jnp.sum(freqs, axis=0) / DEMES
    centered = freqs - mean
    rows = centered.reshape(DEMES * GENS, LOCI)
    gram = lax.dot_general(rows.astype(jnp.float32), rows.astype(jnp.float32), (((0,), (0,)), ((), ())), precision=lax.Precision.HIGHEST, preferred_element_type=jnp.float32)
    gram = gram * (1.0 / (DEMES * GENS))
    basis = start_basis
    for step in range(ITERS):
        basis = orthonormal(jnp.dot(gram.astype(jnp.float32), basis.astype(jnp.float32), precision=lax.Precision.HIGHEST, preferred_element_type=jnp.float32))
    core = jnp.dot(rows.astype(jnp.float32), basis.astype(jnp.float32), precision=lax.Precision.HIGHEST, preferred_element_type=jnp.float32)
    return (core.reshape(DEMES, GENS, RANK), basis)
```

```python
import functools

import jax
import jax.numpy as jnp
from jax import lax
from jax.experimental import pallas as pl
from jax.experimental.pallas import tpu as pltpu
from jax.sharding import PartitionSpec as P

ITERS = 4
MESH = pl.DeviceIdType.MESH
HIGHEST = lax.Precision.HIGHEST
F32 = jnp.float32
BF16 = jnp.bfloat16
LANES = 128


def dot(a, b):
    return jnp.dot(a, b, precision=HIGHEST, preferred_element_type=F32)


def tdot(a, b):
    return lax.dot_general(
        a, b, (((0,), (0,)), ((), ())), precision=HIGHEST, preferred_element_type=F32
    )


def tdot16(a, b):
    return lax.dot_general(a, b, (((0,), (0,)), ((), ())), preferred_element_type=F32)


def split(a):
    hi = a.astype(BF16)
    return hi, (a - hi.astype(F32)).astype(BF16)


def pairs(loci):
    tiles = loci // LANES
    return [(i, j) for i in range(tiles) for j in range(i, tiles)]


def gram_kernel(count, x_ref, g_ref, mu_ref, shift, total, same, cross):
    step = pl.program_id(0)
    demes, gens, loci = x_ref.shape
    half = loci // 2

    @pl.when(step == 0)
    def _():
        shift[...] = jnp.sum(x_ref[...], axis=0) * (1.0 / demes)
        total[...] = jnp.zeros_like(total)
        same[...] = jnp.zeros_like(same)
        cross[...] = jnp.zeros_like(cross)

    moved = x_ref[...] - shift[...][None]
    total[...] += jnp.sum(moved, axis=0)
    hi, lo = split(moved.reshape(demes * gens, loci))
    for i in range(2):
        left = hi[:, i * half : (i + 1) * half]
        same[i * half : (i + 1) * half, i * half :] += tdot16(left, hi[:, i * half :])
        cross[i * half : (i + 1) * half, :] += tdot16(left, lo)

    @pl.when(step == pl.num_programs(0) - 1)
    def _():
        rest = total[...] * (1.0 / count)
        mean = shift[...] + rest
        for j in range(loci // LANES):
            mu_ref[j * gens : (j + 1) * gens, :] = mean[:, j * LANES : (j + 1) * LANES]
        for index, (i, j) in enumerate(pairs(loci)):
            rows, cols = slice(i * LANES, (i + 1) * LANES), slice(j * LANES, (j + 1) * LANES)
            block = same[rows, cols] + cross[rows, cols] + cross[cols, rows].T
            block = block - tdot(rest[:, rows], rest[:, cols]) * count
            g_ref[index * LANES : (index + 1) * LANES, :] = block
        used = len(pairs(loci)) * LANES
        if used < g_ref.shape[0]:
            g_ref[used:, :] = jnp.zeros((g_ref.shape[0] - used, LANES), F32)


def local_gram(freqs, packed):
    demes, gens, loci = freqs.shape
    tile = min(32, demes)
    return pl.pallas_call(
        functools.partial(gram_kernel, demes),
        grid=(demes // tile,),
        in_specs=[pl.BlockSpec((tile, gens, loci), lambda i: (i, 0, 0))],
        out_specs=[
            pl.BlockSpec((packed, LANES), lambda i: (0, 0)),
            pl.BlockSpec((gens * loci // LANES, LANES), lambda i: (0, 0)),
        ],
        out_shape=[
            jax.ShapeDtypeStruct((packed, LANES), F32),
            jax.ShapeDtypeStruct((gens * loci // LANES, LANES), F32),
        ],
        scratch_shapes=[
            pltpu.VMEM((gens, loci), F32),
            pltpu.VMEM((gens, loci), F32),
            pltpu.VMEM((loci, loci), F32),
            pltpu.VMEM((loci, loci), F32),
        ],
        compiler_params=pltpu.CompilerParams(vmem_limit_bytes=40 * 2**20),
        name="local_gram",
    )(freqs)


def reduce_kernel(
    count, nd, nx, loci, g_ref, mu_ref, out_ref, mean_ref,
    acc, got_core, got_x, got_deme, full, got_mu, mean,
    send_core, recv_core, send_x, recv_x, send_deme, recv_deme, send_mu, recv_mu,
    send_core2, recv_core2, send_x2, recv_x2, send_deme2, recv_deme2, send_mu2, recv_mu2,
):
    deme = lax.axis_index("deme")
    gen = lax.axis_index("gen")
    x, core = gen // 2, gen % 2

    def at_core():
        return (deme, x * 2 + (1 - core))

    def at_x(k):
        return (deme, ((x + k) % nx) * 2 + core)

    def at_deme(k):
        return ((deme + k) % nd, gen)

    peers = [at_core()] + [at_x(k) for k in range(1, nx)] + [at_deme(k) for k in range(1, nd)]
    barrier = pltpu.get_barrier_semaphore()
    for peer in peers:
        pl.semaphore_signal(barrier, inc=1, device_id=peer, device_id_type=MESH)
    pl.semaphore_wait(barrier, len(peers))

    def copy(src, dst, send, recv, peer):
        return pltpu.make_async_remote_copy(
            src_ref=src, dst_ref=dst, send_sem=send, recv_sem=recv,
            device_id=peer, device_id_type=MESH,
        )

    def run(copies):
        for c in copies:
            c.start()
        for c in copies:
            c.wait()

    def rows(start, size):
        return pl.ds(pl.multiple_of(start, 8), size)

    mrows = mu_ref.shape[0] // nd
    run([
        copy(mu_ref.at[rows((deme + k) % nd * mrows, mrows)], got_mu.at[k - 1],
             send_mu.at[k - 1], recv_mu.at[k - 1], at_deme(k))
        for k in range(1, nd)
    ])
    own = rows(deme * mrows, mrows)
    value = mu_ref[own, :]
    for k in range(1, nd):
        value = value + got_mu[k - 1]
    mean[own, :] = value * (1.0 / nd)
    run([
        copy(mean.at[own], mean.at[own], send_mu2.at[k - 1], recv_mu2.at[k - 1], at_deme(k))
        for k in range(1, nd)
    ])
    mean_ref[...] = mean[...]

    gens = mu_ref.shape[0] // (loci // LANES)
    apart = mean[...] - mu_ref[...]
    for index, (i, j) in enumerate(pairs(loci)):
        at = slice(index * LANES, (index + 1) * LANES)
        acc[at, :] = g_ref[at, :] + count * tdot(
            apart[i * gens : (i + 1) * gens], apart[j * gens : (j + 1) * gens]
        )
    used = len(pairs(loci)) * LANES
    if used < acc.shape[0]:
        acc[used:, :] = g_ref[used:, :]

    size0 = acc.shape[0] // 2
    size1 = size0 // nx
    size2 = size1 // nd
    run([copy(acc.at[rows((1 - core) * size0, size0)], got_core, send_core, recv_core, at_core())])
    at0 = core * size0
    acc[rows(at0, size0), :] += got_core[...]
    run([
        copy(acc.at[rows(at0 + (x + k) % nx * size1, size1)], got_x.at[k - 1],
             send_x.at[k - 1], recv_x.at[k - 1], at_x(k))
        for k in range(1, nx)
    ])
    at1 = at0 + x * size1
    value = acc[rows(at1, size1), :]
    for k in range(1, nx):
        value = value + got_x[k - 1]
    acc[rows(at1, size1), :] = value
    run([
        copy(acc.at[rows(at1 + (deme + k) % nd * size2, size2)], got_deme.at[k - 1],
             send_deme.at[k - 1], recv_deme.at[k - 1], at_deme(k))
        for k in range(1, nd)
    ])
    at2 = at1 + deme * size2
    value = acc[rows(at2, size2), :]
    for k in range(1, nd):
        value = value + got_deme[k - 1]
    full[rows(at2, size2), :] = value

    mine = full.at[rows(at2, size2)]
    run([
        copy(mine, mine, send_deme2.at[k - 1], recv_deme2.at[k - 1], at_deme(k))
        for k in range(1, nd)
    ])
    mine = full.at[rows(at1, size1)]
    run([copy(mine, mine, send_x2.at[k - 1], recv_x2.at[k - 1], at_x(k)) for k in range(1, nx)])
    mine = full.at[rows(at0, size0)]
    run([copy(mine, mine, send_core2, recv_core2, at_core())])
    out_ref[...] = full[...]


def reduce_all(gram, mu, count, nd, nx, loci):
    packed = gram.shape[0]
    size1 = packed // 2 // nx
    dma = pltpu.SemaphoreType.DMA
    sems = [dma, dma] + [dma((max(nx - 1, 1),))] * 2 + [dma((nd - 1,))] * 4
    return pl.pallas_call(
        functools.partial(reduce_kernel, count, nd, nx, loci),
        in_specs=[pl.BlockSpec(memory_space=pltpu.VMEM)] * 2,
        out_specs=[pl.BlockSpec(memory_space=pltpu.VMEM)] * 2,
        out_shape=[jax.ShapeDtypeStruct(gram.shape, F32), jax.ShapeDtypeStruct(mu.shape, F32)],
        scratch_shapes=[
            pltpu.VMEM((packed, LANES), F32),
            pltpu.VMEM((packed // 2, LANES), F32),
            pltpu.VMEM((max(nx - 1, 1), size1, LANES), F32),
            pltpu.VMEM((nd - 1, size1 // nd, LANES), F32),
            pltpu.VMEM((packed, LANES), F32),
            pltpu.VMEM((nd - 1, mu.shape[0] // nd, LANES), F32),
            pltpu.VMEM(mu.shape, F32),
        ] + sems + sems,
        compiler_params=pltpu.CompilerParams(
            collective_id=0, has_side_effects=True, vmem_limit_bytes=40 * 2**20
        ),
        name="reduce_all",
    )(gram, mu)


def inverse_lower(work, out):
    size = out.shape[0]
    lane = lax.broadcasted_iota(jnp.int32, (8, size), 1)

    def spread(row):
        return jnp.broadcast_to(row, (8, size))

    for panel in range(size // 8):
        first = panel * 8
        block = work[first : first + 8, :]
        columns = [
            jnp.broadcast_to(block[:, first + k : first + k + 1], (8, size)) for k in range(8)
        ]
        entry = {(i, k): spread(columns[k][i : i + 1, :]) for k in range(8) for i in range(k, 8)}
        scale = {}
        for k in range(8):
            scale[k] = lax.rsqrt(entry[k, k])
            for i in range(k + 1, 8):
                entry[i, k] = entry[i, k] * scale[k]
            for j in range(k + 1, 8):
                for i in range(j, 8):
                    entry[i, j] = entry[i, j] - entry[i, k] * entry[j, k]
        left, right = [], []
        for k in range(8):
            a, b = spread(block[k : k + 1, :size]), spread(block[k : k + 1, size:])
            for i in range(k):
                a = a - entry[k, i] * left[i]
                b = b - entry[k, i] * right[i]
            left.append(a * scale[k])
            right.append(b * scale[k])
        sub = lax.broadcasted_iota(jnp.int32, (8, size), 0)
        lefts, rights = left[0], right[0]
        for k in range(1, 8):
            lefts = jnp.where(sub == k, left[k], lefts)
            rights = jnp.where(sub == k, right[k], rights)
        out[first : first + 8, :] = rights
        if first + 8 < size:
            later = jnp.where(lane >= first + 8, lefts, 0.0)
            both = jnp.concatenate([lefts, rights], axis=1)
            work[...] = work[...] - tdot(later, both)


def basis_kernel(scale, g_ref, start_ref, out_ref, gram, work, inverse):
    loci, rank = start_ref.shape
    for index, (i, j) in enumerate(pairs(loci)):
        block = g_ref[index * LANES : (index + 1) * LANES, :] * scale
        gram[i * LANES : (i + 1) * LANES, j * LANES : (j + 1) * LANES] = block
        if i != j:
            gram[j * LANES : (j + 1) * LANES, i * LANES : (i + 1) * LANES] = block.T
    out_ref[...] = start_ref[...]
    row = lax.broadcasted_iota(jnp.int32, (rank, rank), 0)
    column = lax.broadcasted_iota(jnp.int32, (rank, rank), 1)

    def step(_, carry):
        z = dot(gram[...], out_ref[...])
        work[:, :rank] = tdot(z, z)
        work[:, rank:] = jnp.where(row == column, 1.0, 0.0)
        inverse_lower(work, inverse)
        out_ref[...] = lax.dot_general(
            z, inverse[...], (((1,), (1,)), ((), ())), precision=HIGHEST,
            preferred_element_type=F32,
        )
        return carry

    lax.fori_loop(0, ITERS, step, 0)


def find_basis(gram, start, scale):
    loci, rank = start.shape
    return pl.pallas_call(
        functools.partial(basis_kernel, scale),
        in_specs=[pl.BlockSpec(memory_space=pltpu.VMEM)] * 2,
        out_specs=pl.BlockSpec(memory_space=pltpu.VMEM),
        out_shape=jax.ShapeDtypeStruct(start.shape, F32),
        scratch_shapes=[
            pltpu.VMEM((loci, loci), F32),
            pltpu.VMEM((rank, 2 * rank), F32),
            pltpu.VMEM((rank, rank), F32),
        ],
        compiler_params=pltpu.CompilerParams(vmem_limit_bytes=40 * 2**20),
        name="find_basis",
    )(gram, start)


def core_kernel(x_ref, mean_ref, factor_ref, out_ref):
    demes, gens, loci = x_ref.shape
    rank = factor_ref.shape[1]
    mean = jnp.concatenate(
        [mean_ref[j * gens : (j + 1) * gens, :] for j in range(loci // LANES)], axis=1
    )
    hi, lo = split((x_ref[...] - mean[None]).reshape(demes * gens, loci))
    fhi, flo = split(factor_ref[...])
    both = jnp.dot(hi, jnp.concatenate([fhi, flo], axis=1), preferred_element_type=F32)
    value = both[:, :rank] + (both[:, rank:] + jnp.dot(lo, fhi, preferred_element_type=F32))
    out_ref[...] = value.reshape(demes, gens, rank)


def find_core(freqs, mean, factor):
    demes, gens, loci = freqs.shape
    rank = factor.shape[1]
    tile = min(32, demes)
    return pl.pallas_call(
        core_kernel,
        grid=(demes // tile,),
        in_specs=[
            pl.BlockSpec((tile, gens, loci), lambda i: (i, 0, 0)),
            pl.BlockSpec(mean.shape, lambda i: (0, 0)),
            pl.BlockSpec(factor.shape, lambda i: (0, 0)),
        ],
        out_specs=pl.BlockSpec((tile, gens, rank), lambda i: (i, 0, 0)),
        out_shape=jax.ShapeDtypeStruct((demes, gens, rank), F32),
        compiler_params=pltpu.CompilerParams(vmem_limit_bytes=40 * 2**20),
        name="find_core",
    )(freqs, mean, factor)


def solution(mesh):
    nd, ng = mesh.shape["deme"], mesh.shape["gen"]
    nx = ng // 2

    def local(freqs, start_basis):
        demes, gens, loci = freqs.shape
        unit = 8 * nd * ng
        packed = -(-len(pairs(loci)) * LANES // unit) * unit
        gram, mu = local_gram(freqs, packed)
        gram, mean = reduce_all(gram, mu, demes, nd, nx, loci)
        scale = 1.0 / (demes * nd * gens * ng)
        factor = find_basis(gram, start_basis, scale)
        return find_core(freqs, mean, factor), factor

    in_specs = (P("deme", "gen", None), P())
    out_specs = (P("deme", "gen", None), P())
    return jax.shard_map(local, mesh=mesh, in_specs=in_specs, out_specs=out_specs, check_vma=False)
```

```python
import functools

import jax
import jax.numpy as jnp
from jax import lax
from jax.experimental import pallas as pl
from jax.experimental.pallas import tpu as pltpu
from jax.sharding import PartitionSpec as P

ITERS = 4
MESH = pl.DeviceIdType.MESH
HIGHEST = lax.Precision.HIGHEST
F32 = jnp.float32
BF16 = jnp.bfloat16
LANES = 128


def dot(a, b):
    return jnp.dot(a, b, precision=HIGHEST, preferred_element_type=F32)


def tdot(a, b):
    return lax.dot_general(
        a, b, (((0,), (0,)), ((), ())), precision=HIGHEST, preferred_element_type=F32
    )


def tdot16(a, b):
    return lax.dot_general(a, b, (((0,), (0,)), ((), ())), preferred_element_type=F32)


def split(a):
    hi = a.astype(BF16)
    return hi, (a - hi.astype(F32)).astype(BF16)


def pairs(loci):
    tiles = loci // LANES
    return [(i, j) for i in range(tiles) for j in range(i, tiles)]


def gram_kernel(count, x_ref, g_ref, mu_ref, shift, total, upper, lower):
    step = pl.program_id(0)
    demes, gens, loci = x_ref.shape
    half = loci // 2

    @pl.when(step == 0)
    def _():
        shift[...] = jnp.sum(x_ref[...], axis=0) * (1.0 / demes)
        total[...] = jnp.zeros_like(total)
        upper[...] = jnp.zeros_like(upper)
        lower[...] = jnp.zeros_like(lower)

    moved = x_ref[...] - shift[...][None]
    total[...] += jnp.sum(moved, axis=0)
    hi, lo = split(moved.reshape(demes * gens, loci))
    upper[...] += tdot16(hi[:, :half], jnp.concatenate([hi, lo], axis=1))
    lower[...] += tdot16(hi[:, half:], jnp.concatenate([hi[:, half:], lo], axis=1))

    def same(i, j):
        if i < half // LANES:
            return upper[i * LANES : (i + 1) * LANES, j * LANES : (j + 1) * LANES]
        return lower[
            i * LANES - half : (i + 1) * LANES - half, j * LANES - half : (j + 1) * LANES - half
        ]

    def cross(i, j):
        if i < half // LANES:
            return upper[i * LANES : (i + 1) * LANES, loci + j * LANES : loci + (j + 1) * LANES]
        return lower[
            i * LANES - half : (i + 1) * LANES - half, half + j * LANES : half + (j + 1) * LANES
        ]

    @pl.when(step == pl.num_programs(0) - 1)
    def _():
        rest = total[...] * (1.0 / count)
        mean = shift[...] + rest
        for j in range(loci // LANES):
            mu_ref[j * gens : (j + 1) * gens, :] = mean[:, j * LANES : (j + 1) * LANES]
        for index, (i, j) in enumerate(pairs(loci)):
            rows, cols = slice(i * LANES, (i + 1) * LANES), slice(j * LANES, (j + 1) * LANES)
            block = same(i, j) + (cross(i, j) + cross(j, i).T)
            block = block - tdot(rest[:, rows], rest[:, cols]) * count
            g_ref[index * LANES : (index + 1) * LANES, :] = block
        used = len(pairs(loci)) * LANES
        if used < g_ref.shape[0]:
            g_ref[used:, :] = jnp.zeros((g_ref.shape[0] - used, LANES), F32)


def local_gram(freqs, packed):
    demes, gens, loci = freqs.shape
    tile = min(32, demes)
    return pl.pallas_call(
        functools.partial(gram_kernel, demes),
        grid=(demes // tile,),
        in_specs=[pl.BlockSpec((tile, gens, loci), lambda i: (i, 0, 0))],
        out_specs=[
            pl.BlockSpec((packed, LANES), lambda i: (0, 0)),
            pl.BlockSpec((gens * loci // LANES, LANES), lambda i: (0, 0)),
        ],
        out_shape=[
            jax.ShapeDtypeStruct((packed, LANES), F32),
            jax.ShapeDtypeStruct((gens * loci // LANES, LANES), F32),
        ],
        scratch_shapes=[
            pltpu.VMEM((gens, loci), F32),
            pltpu.VMEM((gens, loci), F32),
            pltpu.VMEM((loci // 2, 2 * loci), F32),
            pltpu.VMEM((loci // 2, loci + loci // 2), F32),
        ],
        compiler_params=pltpu.CompilerParams(vmem_limit_bytes=40 * 2**20),
        name="local_gram",
    )(freqs)


def reduce_kernel(
    count, nd, nx, loci, g_ref, mu_ref, out_ref, mean_ref,
    acc, got_core, got_x, got_deme, full, got_mu, mean,
    send_core, recv_core, send_x, recv_x, send_deme, recv_deme, send_mu, recv_mu,
    send_core2, recv_core2, send_x2, recv_x2, send_deme2, recv_deme2, send_mu2, recv_mu2,
):
    deme = lax.axis_index("deme")
    gen = lax.axis_index("gen")
    x, core = gen // 2, gen % 2

    def at_core():
        return (deme, x * 2 + (1 - core))

    def at_x(k):
        return (deme, ((x + k) % nx) * 2 + core)

    def at_deme(k):
        return ((deme + k) % nd, gen)

    peers = [at_core()] + [at_x(k) for k in range(1, nx)] + [at_deme(k) for k in range(1, nd)]
    barrier = pltpu.get_barrier_semaphore()
    for peer in peers:
        pl.semaphore_signal(barrier, inc=1, device_id=peer, device_id_type=MESH)
    pl.semaphore_wait(barrier, len(peers))

    def copy(src, dst, send, recv, peer):
        return pltpu.make_async_remote_copy(
            src_ref=src, dst_ref=dst, send_sem=send, recv_sem=recv,
            device_id=peer, device_id_type=MESH,
        )

    def run(copies):
        for c in copies:
            c.start()
        for c in copies:
            c.wait()

    def rows(start, size):
        return pl.ds(pl.multiple_of(start, 8), size)

    mrows = mu_ref.shape[0] // nd
    run([
        copy(mu_ref.at[rows((deme + k) % nd * mrows, mrows)], got_mu.at[k - 1],
             send_mu.at[k - 1], recv_mu.at[k - 1], at_deme(k))
        for k in range(1, nd)
    ])
    own = rows(deme * mrows, mrows)
    value = mu_ref[own, :]
    for k in range(1, nd):
        value = value + got_mu[k - 1]
    mean[own, :] = value * (1.0 / nd)
    run([
        copy(mean.at[own], mean.at[own], send_mu2.at[k - 1], recv_mu2.at[k - 1], at_deme(k))
        for k in range(1, nd)
    ])
    mean_ref[...] = mean[...]

    gens = mu_ref.shape[0] // (loci // LANES)
    apart = mean[...] - mu_ref[...]
    for index, (i, j) in enumerate(pairs(loci)):
        at = slice(index * LANES, (index + 1) * LANES)
        acc[at, :] = g_ref[at, :] + count * tdot(
            apart[i * gens : (i + 1) * gens], apart[j * gens : (j + 1) * gens]
        )
    used = len(pairs(loci)) * LANES
    if used < acc.shape[0]:
        acc[used:, :] = g_ref[used:, :]

    size0 = acc.shape[0] // 2
    size1 = size0 // nx
    size2 = size1 // nd
    run([copy(acc.at[rows((1 - core) * size0, size0)], got_core, send_core, recv_core, at_core())])
    at0 = core * size0
    acc[rows(at0, size0), :] += got_core[...]
    run([
        copy(acc.at[rows(at0 + (x + k) % nx * size1, size1)], got_x.at[k - 1],
             send_x.at[k - 1], recv_x.at[k - 1], at_x(k))
        for k in range(1, nx)
    ])
    at1 = at0 + x * size1
    value = acc[rows(at1, size1), :]
    for k in range(1, nx):
        value = value + got_x[k - 1]
    acc[rows(at1, size1), :] = value
    run([
        copy(acc.at[rows(at1 + (deme + k) % nd * size2, size2)], got_deme.at[k - 1],
             send_deme.at[k - 1], recv_deme.at[k - 1], at_deme(k))
        for k in range(1, nd)
    ])
    at2 = at1 + deme * size2
    value = acc[rows(at2, size2), :]
    for k in range(1, nd):
        value = value + got_deme[k - 1]
    full[rows(at2, size2), :] = value

    mine = full.at[rows(at2, size2)]
    run([
        copy(mine, mine, send_deme2.at[k - 1], recv_deme2.at[k - 1], at_deme(k))
        for k in range(1, nd)
    ])
    mine = full.at[rows(at1, size1)]
    run([copy(mine, mine, send_x2.at[k - 1], recv_x2.at[k - 1], at_x(k)) for k in range(1, nx)])
    mine = full.at[rows(at0, size0)]
    run([copy(mine, mine, send_core2, recv_core2, at_core())])
    out_ref[...] = full[...]


def reduce_all(gram, mu, count, nd, nx, loci):
    packed = gram.shape[0]
    size1 = packed // 2 // nx
    dma = pltpu.SemaphoreType.DMA
    sems = [dma, dma] + [dma((max(nx - 1, 1),))] * 2 + [dma((nd - 1,))] * 4
    return pl.pallas_call(
        functools.partial(reduce_kernel, count, nd, nx, loci),
        in_specs=[pl.BlockSpec(memory_space=pltpu.VMEM)] * 2,
        out_specs=[pl.BlockSpec(memory_space=pltpu.VMEM)] * 2,
        out_shape=[jax.ShapeDtypeStruct(gram.shape, F32), jax.ShapeDtypeStruct(mu.shape, F32)],
        scratch_shapes=[
            pltpu.VMEM((packed, LANES), F32),
            pltpu.VMEM((packed // 2, LANES), F32),
            pltpu.VMEM((max(nx - 1, 1), size1, LANES), F32),
            pltpu.VMEM((nd - 1, size1 // nd, LANES), F32),
            pltpu.VMEM((packed, LANES), F32),
            pltpu.VMEM((nd - 1, mu.shape[0] // nd, LANES), F32),
            pltpu.VMEM(mu.shape, F32),
        ] + sems + sems,
        compiler_params=pltpu.CompilerParams(
            collective_id=0, has_side_effects=True, vmem_limit_bytes=40 * 2**20
        ),
        name="reduce_all",
    )(gram, mu)


def inverse_lower(matrix):
    size = matrix.shape[0]
    shape = (8, size)
    lane = lax.broadcasted_iota(jnp.int32, shape, 1)
    sub = lax.broadcasted_iota(jnp.int32, shape, 0)

    def spread(row):
        return jnp.broadcast_to(row, shape)

    tiles = [matrix[t * 8 : t * 8 + 8, :] for t in range(size // 8)]
    done = []
    for panel in range(len(tiles)):
        first = panel * 8
        inside = (lane >= first) & (lane < first + 8)
        columns = [
            [jnp.broadcast_to(tile[:, first + k : first + k + 1], shape) for k in range(8)]
            for tile in tiles[panel:]
        ]
        entry = {(i, k): spread(columns[0][k][i : i + 1, :]) for k in range(8) for i in range(k, 8)}
        base = jnp.where(inside, jnp.where(lane == first + sub, 1.0, 0.0), tiles[panel])
        scale, rows = [], []
        for k in range(8):
            scale.append(lax.rsqrt(entry[k, k]))
            for i in range(k + 1, 8):
                entry[i, k] = entry[i, k] * scale[k]
            for j in range(k + 1, 8):
                for i in range(j, 8):
                    entry[i, j] = entry[i, j] - entry[i, k] * entry[j, k]
        for k in range(8):
            row = spread(base[k : k + 1, :])
            for i in range(k):
                row = row - entry[k, i] * rows[i]
            rows.append(row * scale[k])
        block = rows[0]
        for k in range(1, 8):
            block = jnp.where(sub == k, rows[k], block)
        done.append(jnp.where(lane < first + 8, block, 0.0))
        for t in range(panel + 1, len(tiles)):
            column = columns[t - panel]
            tile = jnp.where(inside, 0.0, tiles[t])
            lower = []
            for k in range(8):
                value = column[k]
                for i in range(k):
                    value = value - lower[i] * entry[k, i]
                lower.append(value * scale[k])
                tile = tile - lower[k] * rows[k]
            tiles[t] = tile
    return jnp.concatenate(done, axis=0)


def split3(a):
    one = a.astype(BF16)
    rest = a - one.astype(F32)
    two = rest.astype(BF16)
    return one, two, (rest - two.astype(F32)).astype(BF16)


def dot16(a, b):
    return jnp.dot(a, b, preferred_element_type=F32)


def basis_kernel(scale, g_ref, start_ref, out_ref, gram1, gram2, gram3):
    loci, rank = start_ref.shape
    for index, (i, j) in enumerate(pairs(loci)):
        block = g_ref[index * LANES : (index + 1) * LANES, :] * scale
        rows, cols = slice(i * LANES, (i + 1) * LANES), slice(j * LANES, (j + 1) * LANES)
        for ref, piece in zip((gram1, gram2, gram3), split3(block)):
            ref[rows, cols] = piece
        if i != j:
            for ref, piece in zip((gram1, gram2, gram3), split3(block.T)):
                ref[cols, rows] = piece
    out_ref[...] = start_ref[...]

    def step(_, carry):
        q1, q2, q3 = split3(out_ref[...])
        both = jnp.concatenate([q1, q2], axis=1)
        large, small = dot16(gram1[...], both), dot16(gram2[...], both)
        rest = dot16(gram1[...], q3) + dot16(gram3[...], q1)
        z = large[:, :rank] + (large[:, rank:] + (small[:, :rank] + (small[:, rank:] + rest)))
        z1, z2, z3 = split3(z)
        both = jnp.concatenate([z1, z2], axis=1)
        square = tdot16(both, both)
        rest = tdot16(z1, z3)
        rest = rest + rest.T + square[rank:, rank:]
        small = square[:rank, :rank] + (square[:rank, rank:] + (square[rank:, :rank] + rest))
        w1, w2, w3 = split3(inverse_lower(small))
        right = jnp.concatenate(
            [jnp.concatenate([w1, w1], axis=1), jnp.concatenate([w2, w2], axis=1)], axis=0
        )
        contract = (((1,), (1,)), ((), ()))
        large = lax.dot_general(both, right, contract, preferred_element_type=F32)
        rest = lax.dot_general(
            jnp.concatenate([z3, z1], axis=1), jnp.concatenate([w1, w3], axis=1), contract,
            preferred_element_type=F32,
        )
        out_ref[...] = large[:, :rank] + (large[:, rank:] + rest)
        return carry

    lax.fori_loop(0, ITERS, step, 0)


def find_basis(gram, start, scale):
    loci, rank = start.shape
    return pl.pallas_call(
        functools.partial(basis_kernel, scale),
        in_specs=[pl.BlockSpec(memory_space=pltpu.VMEM)] * 2,
        out_specs=pl.BlockSpec(memory_space=pltpu.VMEM),
        out_shape=jax.ShapeDtypeStruct(start.shape, F32),
        scratch_shapes=[
            pltpu.VMEM((loci, loci), BF16),
            pltpu.VMEM((loci, loci), BF16),
            pltpu.VMEM((loci, loci), BF16),
        ],
        compiler_params=pltpu.CompilerParams(vmem_limit_bytes=40 * 2**20),
        name="find_basis",
    )(gram, start)


def core_kernel(x_ref, mean_ref, factor_ref, out_ref):
    demes, gens, loci = x_ref.shape
    rank = factor_ref.shape[1]
    mean = jnp.concatenate(
        [mean_ref[j * gens : (j + 1) * gens, :] for j in range(loci // LANES)], axis=1
    )
    fhi, flo = split(factor_ref[...])
    pieces = jnp.concatenate([fhi, flo], axis=1)
    part = 8 if demes % 8 == 0 else demes
    for at in range(0, demes, part):
        hi, lo = split((x_ref[at : at + part] - mean[None]).reshape(part * gens, loci))
        both = dot16(hi, pieces)
        value = both[:, :rank] + (both[:, rank:] + dot16(lo, fhi))
        out_ref[at : at + part] = value.reshape(part, gens, rank)


def find_core(freqs, mean, factor):
    demes, gens, loci = freqs.shape
    rank = factor.shape[1]
    tile = min(32, demes)
    return pl.pallas_call(
        core_kernel,
        grid=(demes // tile,),
        in_specs=[
            pl.BlockSpec((tile, gens, loci), lambda i: (i, 0, 0)),
            pl.BlockSpec(mean.shape, lambda i: (0, 0)),
            pl.BlockSpec(factor.shape, lambda i: (0, 0)),
        ],
        out_specs=pl.BlockSpec((tile, gens, rank), lambda i: (i, 0, 0)),
        out_shape=jax.ShapeDtypeStruct((demes, gens, rank), F32),
        compiler_params=pltpu.CompilerParams(vmem_limit_bytes=40 * 2**20),
        name="find_core",
    )(freqs, mean, factor)


def solution(mesh):
    nd, ng = mesh.shape["deme"], mesh.shape["gen"]
    nx = ng // 2

    def local(freqs, start_basis):
        demes, gens, loci = freqs.shape
        unit = 8 * nd * ng
        packed = -(-len(pairs(loci)) * LANES // unit) * unit
        gram, mu = local_gram(freqs, packed)
        gram, mean = reduce_all(gram, mu, demes, nd, nx, loci)
        scale = 1.0 / (demes * nd * gens * ng)
        factor = find_basis(gram, start_basis, scale)
        return find_core(freqs, mean, factor), factor

    in_specs = (P("deme", "gen", None), P())
    out_specs = (P("deme", "gen", None), P())
    return jax.shard_map(local, mesh=mesh, in_specs=in_specs, out_specs=out_specs, check_vma=False)
```

```python
import functools

import jax
import jax.numpy as jnp
from jax import lax
from jax.experimental import pallas as pl
from jax.experimental.pallas import tpu as pltpu
from jax.sharding import PartitionSpec as P

ITERS = 4
MESH = pl.DeviceIdType.MESH
HIGHEST = lax.Precision.HIGHEST
F32 = jnp.float32
BF16 = jnp.bfloat16
LANES = 128


def dot(a, b):
    return jnp.dot(a, b, precision=HIGHEST, preferred_element_type=F32)


def tdot(a, b):
    return lax.dot_general(
        a, b, (((0,), (0,)), ((), ())), precision=HIGHEST, preferred_element_type=F32
    )


def tdot16(a, b):
    return lax.dot_general(a, b, (((0,), (0,)), ((), ())), preferred_element_type=F32)


def split(a):
    hi = a.astype(BF16)
    return hi, (a - hi.astype(F32)).astype(BF16)


def pairs(loci):
    tiles = loci // LANES
    return [(i, j) for i in range(tiles) for j in range(i, tiles)]


def chains(unit):
    first = unit // 16 * 8
    return [first, unit - first] if first else [unit]


def gram_kernel(
    nd, nx, x_ref, out_ref, mean_ref, kept,
    shift, total, upper, lower, mu, mean, got_mu, acc, got_core, got_x, got_deme, full,
    load, send_mu, recv_mu, send_mu2, recv_mu2,
    send_core, recv_core, send_x, recv_x, send_deme, recv_deme,
    send_core2, recv_core2, send_x2, recv_x2, send_deme2, recv_deme2,
):
    demes, gens, loci = x_ref.shape
    half = loci // 2
    parts = load.shape[0]
    tile = demes // parts
    deme = lax.axis_index("deme")
    gen = lax.axis_index("gen")
    x, core = gen // 2, gen % 2

    def at_core():
        return (deme, x * 2 + (1 - core))

    def at_x(k):
        return (deme, ((x + k) % nx) * 2 + core)

    def at_deme(k):
        return ((deme + k) % nd, gen)

    peers = [at_core()] + [at_x(k) for k in range(1, nx)] + [at_deme(k) for k in range(1, nd)]
    barrier = pltpu.get_barrier_semaphore()
    for peer in peers:
        pl.semaphore_signal(barrier, inc=1, device_id=peer, device_id_type=MESH)

    def copy(src, dst, send, recv, peer):
        return pltpu.make_async_remote_copy(
            src_ref=src, dst_ref=dst, send_sem=send, recv_sem=recv,
            device_id=peer, device_id_type=MESH,
        )

    def start(copies):
        for c in copies:
            c.start()
        return copies

    def wait(copies):
        for c in copies:
            c.wait()

    def rows(first, size):
        return pl.ds(pl.multiple_of(first, 8), size)

    loads = start([
        pltpu.make_async_copy(
            x_ref.at[pl.ds(i * tile, tile)], kept.at[pl.ds(i * tile, tile)], load.at[i]
        )
        for i in range(parts)
    ])

    def add_sum(i):
        loads[i].wait()
        total[...] += jnp.sum(kept[i * tile : (i + 1) * tile], axis=0)

    def add_gram(i):
        moved = kept[pl.ds(i * tile, tile)] - shift[...][None]
        hi, lo = split(moved.reshape(tile * gens, loci))
        upper[...] += tdot16(hi[:, :half], jnp.concatenate([hi, lo], axis=1))
        lower[...] += tdot16(hi[:, half:], jnp.concatenate([hi[:, half:], lo], axis=1))

    def grams(first, last):
        def body(i, carry):
            add_gram(i)
            return carry

        lax.fori_loop(first, last, body, 0)

    total[...] = jnp.zeros_like(total)
    upper[...] = jnp.zeros_like(upper)
    lower[...] = jnp.zeros_like(lower)
    add_sum(0)
    shift[...] = total[...] * (1.0 / tile)
    early = parts // 4
    for i in range(1, parts // 2):
        add_sum(i)
    grams(0, early)
    for i in range(max(parts // 2, 1), parts):
        add_sum(i)
    tiles = loci // LANES
    own_mean = total[...] * (1.0 / demes)
    for j in range(tiles):
        mu[j * gens : (j + 1) * gens, :] = own_mean[:, j * LANES : (j + 1) * LANES]
    rest = own_mean - shift[...]

    pl.semaphore_wait(barrier, len(peers))
    mrows = mu.shape[0] // nd
    sent = start([
        copy(mu.at[rows((deme + k) % nd * mrows, mrows)], got_mu.at[k - 1],
             send_mu.at[k - 1], recv_mu.at[k - 1], at_deme(k))
        for k in range(1, nd)
    ])
    middle = (early + parts + 1) // 2
    grams(early, middle)
    wait(sent)
    own = rows(deme * mrows, mrows)
    value = mu[own, :]
    for k in range(1, nd):
        value = value + got_mu[k - 1]
    mean[own, :] = value * (1.0 / nd)
    sent = start([
        copy(mean.at[own], mean.at[own], send_mu2.at[k - 1], recv_mu2.at[k - 1], at_deme(k))
        for k in range(1, nd)
    ])
    grams(middle, parts)
    wait(sent)
    mean_ref[...] = mean[...]

    def same(i, j):
        if i < half // LANES:
            return upper[i * LANES : (i + 1) * LANES, j * LANES : (j + 1) * LANES]
        return lower[
            i * LANES - half : (i + 1) * LANES - half, j * LANES - half : (j + 1) * LANES - half
        ]

    def cross(i, j):
        if i < half // LANES:
            return upper[i * LANES : (i + 1) * LANES, loci + j * LANES : loci + (j + 1) * LANES]
        return lower[
            i * LANES - half : (i + 1) * LANES - half, half + j * LANES : half + (j + 1) * LANES
        ]

    apart = [
        mean[j * gens : (j + 1) * gens, :] - mu[j * gens : (j + 1) * gens, :] for j in range(tiles)
    ]
    moved = [rest[:, j * LANES : (j + 1) * LANES] for j in range(tiles)]
    left = [jnp.concatenate([a, b], axis=0) for a, b in zip(apart, moved)]
    right = [jnp.concatenate([a, -b], axis=0) for a, b in zip(apart, moved)]
    for index, (i, j) in enumerate(pairs(loci)):
        block = same(i, j) + (cross(i, j) + cross(j, i).T)
        acc[index * LANES : (index + 1) * LANES, :] = block + demes * tdot(left[i], right[j])
    used = len(pairs(loci)) * LANES
    if used < acc.shape[0]:
        acc[used:, :] = jnp.zeros((acc.shape[0] - used, LANES), F32)

    def steps(c, base, unit):
        size1 = unit * nd
        size0 = size1 * nx
        at0 = base * nd * nx * 2 + core * size0
        other0 = base * nd * nx * 2 + (1 - core) * size0
        at1 = at0 + x * size1
        at2 = at1 + deme * unit
        part0 = got_core.at[pl.ds(base * nd * nx, size0)]
        part1 = [got_x.at[k - 1, pl.ds(base * nd, size1)] for k in range(1, nx)]
        part2 = [got_deme.at[k - 1, pl.ds(base, unit)] for k in range(1, nd)]
        sent = start([
            copy(acc.at[rows(other0, size0)], part0, send_core.at[c], recv_core.at[c], at_core())
        ])
        yield
        wait(sent)
        acc[rows(at0, size0), :] += part0[...]
        sent = start([
            copy(acc.at[rows(at0 + (x + k) % nx * size1, size1)], part1[k - 1],
                 send_x.at[c, k - 1], recv_x.at[c, k - 1], at_x(k))
            for k in range(1, nx)
        ])
        yield
        wait(sent)
        value = acc[rows(at1, size1), :]
        for part in part1:
            value = value + part[...]
        acc[rows(at1, size1), :] = value
        sent = start([
            copy(acc.at[rows(at1 + (deme + k) % nd * unit, unit)], part2[k - 1],
                 send_deme.at[c, k - 1], recv_deme.at[c, k - 1], at_deme(k))
            for k in range(1, nd)
        ])
        yield
        wait(sent)
        value = acc[rows(at2, unit), :]
        for part in part2:
            value = value + part[...]
        full[rows(at2, unit), :] = value
        mine = full.at[rows(at2, unit)]
        sent = start([
            copy(mine, mine, send_deme2.at[c, k - 1], recv_deme2.at[c, k - 1], at_deme(k))
            for k in range(1, nd)
        ])
        yield
        wait(sent)
        mine1 = full.at[rows(at1, size1)]
        sent = start([
            copy(mine1, mine1, send_x2.at[c, k - 1], recv_x2.at[c, k - 1], at_x(k))
            for k in range(1, nx)
        ])
        yield
        wait(sent)
        mine0 = full.at[rows(at0, size0)]
        sent = start([copy(mine0, mine0, send_core2.at[c], recv_core2.at[c], at_core())])
        yield
        wait(sent)
        yield

    running, base = [], 0
    for c, unit in enumerate(chains(got_deme.shape[1])):
        running.append(steps(c, base, unit))
        base += unit
    for _ in range(7):
        for chain in running:
            next(chain)
    out_ref[...] = full[...]


def sum_gram(freqs, packed, nd, nx):
    demes, gens, loci = freqs.shape
    parts = 8 if demes % 8 == 0 else 1
    unit = packed // (2 * nx * nd)
    count = len(chains(unit))
    mshape = (gens * loci // LANES, LANES)
    far = max(nx - 1, 1)
    dma = pltpu.SemaphoreType.DMA
    sems = [dma((count,))] * 2 + [dma((count, far))] * 2 + [dma((count, nd - 1))] * 2
    vmem = pl.BlockSpec(memory_space=pltpu.VMEM)
    return pl.pallas_call(
        functools.partial(gram_kernel, nd, nx),
        in_specs=[pl.BlockSpec(memory_space=pl.ANY)],
        out_specs=[vmem, vmem, vmem],
        out_shape=[
            jax.ShapeDtypeStruct((packed, LANES), F32),
            jax.ShapeDtypeStruct(mshape, F32),
            pltpu.VMEM(freqs.shape, F32),
        ],
        scratch_shapes=[
            pltpu.VMEM((gens, loci), F32),
            pltpu.VMEM((gens, loci), F32),
            pltpu.VMEM((loci // 2, 2 * loci), F32),
            pltpu.VMEM((loci // 2, loci + loci // 2), F32),
            pltpu.VMEM(mshape, F32),
            pltpu.VMEM(mshape, F32),
            pltpu.VMEM((nd - 1, mshape[0] // nd, LANES), F32),
            pltpu.VMEM((packed, LANES), F32),
            pltpu.VMEM((packed // 2, LANES), F32),
            pltpu.VMEM((far, unit * nd, LANES), F32),
            pltpu.VMEM((nd - 1, unit, LANES), F32),
            pltpu.VMEM((packed, LANES), F32),
            dma((parts,)),
        ] + [dma((nd - 1,))] * 4 + sems + sems,
        compiler_params=pltpu.CompilerParams(
            collective_id=0, has_side_effects=True, vmem_limit_bytes=30 * 2**20
        ),
        name="sum_gram",
    )(freqs)


def inverse_lower(matrix):
    size = matrix.shape[0]
    shape = (8, size)
    lane = lax.broadcasted_iota(jnp.int32, shape, 1)
    sub = lax.broadcasted_iota(jnp.int32, shape, 0)

    def spread(row):
        return jnp.broadcast_to(row, shape)

    tiles = [matrix[t * 8 : t * 8 + 8, :] for t in range(size // 8)]
    done = []
    for panel in range(len(tiles)):
        first = panel * 8
        inside = (lane >= first) & (lane < first + 8)
        columns = [
            [jnp.broadcast_to(tile[:, first + k : first + k + 1], shape) for k in range(8)]
            for tile in tiles[panel:]
        ]
        entry = {(i, k): spread(columns[0][k][i : i + 1, :]) for k in range(8) for i in range(k, 8)}
        base = jnp.where(inside, jnp.where(lane == first + sub, 1.0, 0.0), tiles[panel])
        scale, rows = [], []
        for k in range(8):
            scale.append(lax.rsqrt(entry[k, k]))
            for i in range(k + 1, 8):
                entry[i, k] = entry[i, k] * scale[k]
            for j in range(k + 1, 8):
                for i in range(j, 8):
                    entry[i, j] = entry[i, j] - entry[i, k] * entry[j, k]
        for k in range(8):
            row = spread(base[k : k + 1, :])
            for i in range(k):
                row = row - entry[k, i] * rows[i]
            rows.append(row * scale[k])
        block = rows[0]
        for k in range(1, 8):
            block = jnp.where(sub == k, rows[k], block)
        done.append(jnp.where(lane < first + 8, block, 0.0))
        for t in range(panel + 1, len(tiles)):
            column = columns[t - panel]
            tile = jnp.where(inside, 0.0, tiles[t])
            lower = []
            for k in range(8):
                value = column[k]
                for i in range(k):
                    value = value - lower[i] * entry[k, i]
                lower.append(value * scale[k])
                tile = tile - lower[k] * rows[k]
            tiles[t] = tile
    return jnp.concatenate(done, axis=0)


def split3(a):
    one = a.astype(BF16)
    rest = a - one.astype(F32)
    two = rest.astype(BF16)
    return one, two, (rest - two.astype(F32)).astype(BF16)


def dot16(a, b):
    return jnp.dot(a, b, preferred_element_type=F32)


def basis_kernel(scale, g_ref, start_ref, out_ref, kept, gram1, gram2, gram3):
    loci, rank = start_ref.shape
    for index, (i, j) in enumerate(pairs(loci)):
        block = g_ref[index * LANES : (index + 1) * LANES, :] * scale
        rows, cols = slice(i * LANES, (i + 1) * LANES), slice(j * LANES, (j + 1) * LANES)
        for ref, piece in zip((gram1, gram2, gram3), split3(block)):
            ref[rows, cols] = piece
        if i != j:
            for ref, piece in zip((gram1, gram2, gram3), split3(block.T)):
                ref[cols, rows] = piece
    out_ref[...] = start_ref[...]

    def step(_, carry):
        q1, q2, q3 = split3(out_ref[...])
        both = jnp.concatenate([q1, q2], axis=1)
        large, small = dot16(gram1[...], both), dot16(gram2[...], both)
        rest = dot16(gram1[...], q3) + dot16(gram3[...], q1)
        z = large[:, :rank] + (large[:, rank:] + (small[:, :rank] + (small[:, rank:] + rest)))
        z1, z2, z3 = split3(z)
        both = jnp.concatenate([z1, z2], axis=1)
        square = tdot16(both, both)
        rest = tdot16(z1, z3)
        rest = rest + rest.T + square[rank:, rank:]
        small = square[:rank, :rank] + (square[:rank, rank:] + (square[rank:, :rank] + rest))
        w1, w2, w3 = split3(inverse_lower(small))
        right = jnp.concatenate(
            [jnp.concatenate([w1, w1], axis=1), jnp.concatenate([w2, w2], axis=1)], axis=0
        )
        contract = (((1,), (1,)), ((), ()))
        large = lax.dot_general(both, right, contract, preferred_element_type=F32)
        rest = lax.dot_general(
            jnp.concatenate([z3, z1], axis=1), jnp.concatenate([w1, w3], axis=1), contract,
            preferred_element_type=F32,
        )
        out_ref[...] = large[:, :rank] + (large[:, rank:] + rest)
        return carry

    lax.fori_loop(0, ITERS, step, 0)
    kept[...] = out_ref[...]


def find_basis(gram, start, scale):
    loci, rank = start.shape
    return pl.pallas_call(
        functools.partial(basis_kernel, scale),
        in_specs=[pl.BlockSpec(memory_space=pltpu.VMEM)] * 2,
        out_specs=[pl.BlockSpec(memory_space=pltpu.VMEM)] * 2,
        out_shape=[jax.ShapeDtypeStruct(start.shape, F32), pltpu.VMEM(start.shape, F32)],
        scratch_shapes=[
            pltpu.VMEM((loci, loci), BF16),
            pltpu.VMEM((loci, loci), BF16),
            pltpu.VMEM((loci, loci), BF16),
        ],
        compiler_params=pltpu.CompilerParams(vmem_limit_bytes=30 * 2**20),
        name="find_basis",
    )(gram, start)


def core_kernel(x_ref, mean_ref, factor_ref, out_ref):
    demes, gens, rank = out_ref.shape
    loci = x_ref.shape[2]
    mean = jnp.concatenate(
        [mean_ref[j * gens : (j + 1) * gens, :] for j in range(loci // LANES)], axis=1
    )
    fhi, flo = split(factor_ref[...])
    pieces = jnp.concatenate([fhi, flo], axis=1)
    part = 8 if demes % 8 == 0 else demes
    first = pl.program_id(0) * demes
    for at in range(0, demes, part):
        hi, lo = split((x_ref[pl.ds(first + at, part)] - mean[None]).reshape(part * gens, loci))
        both = dot16(hi, pieces)
        value = both[:, :rank] + (both[:, rank:] + dot16(lo, fhi))
        out_ref[at : at + part] = value.reshape(part, gens, rank)


def find_core(freqs, mean, factor):
    demes, gens, loci = freqs.shape
    rank = factor.shape[1]
    tile = 32 if demes % 32 == 0 else demes
    vmem = pl.BlockSpec(memory_space=pltpu.VMEM)
    return pl.pallas_call(
        core_kernel,
        grid=(demes // tile,),
        in_specs=[vmem, vmem, vmem],
        out_specs=pl.BlockSpec((tile, gens, rank), lambda i: (i, 0, 0)),
        out_shape=jax.ShapeDtypeStruct((demes, gens, rank), F32),
        compiler_params=pltpu.CompilerParams(vmem_limit_bytes=30 * 2**20),
        name="find_core",
    )(pltpu.with_memory_space_constraint(freqs, pltpu.VMEM), mean, factor)


def solution(mesh):
    nd, ng = mesh.shape["deme"], mesh.shape["gen"]
    nx = ng // 2

    def local(freqs, start_basis):
        demes, gens, loci = freqs.shape
        unit = 8 * nd * ng
        packed = -(-len(pairs(loci)) * LANES // unit) * unit
        gram, mean, kept = sum_gram(freqs, packed, nd, nx)
        scale = 1.0 / (demes * nd * gens * ng)
        factor, near = find_basis(gram, start_basis, scale)
        return find_core(kept, mean, near), factor

    in_specs = (P("deme", "gen", None), P())
    out_specs = (P("deme", "gen", None), P())
    return jax.shard_map(local, mesh=mesh, in_specs=in_specs, out_specs=out_specs, check_vma=False)
```

```python
import functools

import jax
import jax.numpy as jnp
from jax import lax
from jax.experimental import pallas as pl
from jax.experimental.pallas import tpu as pltpu
from jax.sharding import PartitionSpec as P

ITERS = 4
MESH = pl.DeviceIdType.MESH
HIGHEST = lax.Precision.HIGHEST
F32 = jnp.float32
BF16 = jnp.bfloat16
LANES = 128


def dot(a, b):
    return jnp.dot(a, b, precision=HIGHEST, preferred_element_type=F32)


def tdot(a, b):
    return lax.dot_general(
        a, b, (((0,), (0,)), ((), ())), precision=HIGHEST, preferred_element_type=F32
    )


def tdot16(a, b):
    return lax.dot_general(a, b, (((0,), (0,)), ((), ())), preferred_element_type=F32)


def split(a):
    hi = a.astype(BF16)
    return hi, (a - hi.astype(F32)).astype(BF16)


def pairs(loci):
    tiles = loci // LANES
    return [(i, j) for i in range(tiles) for j in range(i, tiles)]


def chains(unit):
    first = unit // 16 * 8
    return [first, unit - first] if first else [unit]


def gram_kernel(
    nd, nx, x_ref, out_ref, offset_ref, hi_ref, lo_ref,
    loaded, shift, total, upper, swapped, lower, mu, mean, got_mu, mu2, mean2, apart,
    acc, got_core, got_x, got_deme, full,
    load, send_mu, recv_mu, send_mean, recv_mean, send_mean2, recv_mean2, send_other, recv_other,
    send_core, recv_core, send_x, recv_x, send_deme, recv_deme,
    send_core2, recv_core2, send_x2, recv_x2, send_deme2, recv_deme2,
):
    demes, gens, loci = x_ref.shape
    half = loci // 2
    parts = load.shape[0]
    tile = demes // parts
    deme = lax.axis_index("deme")
    gen = lax.axis_index("gen")
    x, core = gen // 2, gen % 2

    def at_core():
        return (deme, x * 2 + (1 - core))

    def at_x(k):
        return (deme, ((x + k) % nx) * 2 + core)

    def at_deme(k):
        return ((deme + k) % nd, gen)

    def at_other(k):
        return ((deme + k) % nd, x * 2 + (1 - core))

    peers = [at_core()] + [at_x(k) for k in range(1, nx)]
    peers += [at(k) for k in range(1, nd) for at in (at_deme, at_other)]
    barrier = pltpu.get_barrier_semaphore()
    for peer in peers:
        pl.semaphore_signal(barrier, inc=1, device_id=peer, device_id_type=MESH)

    def copy(src, dst, send, recv, peer):
        return pltpu.make_async_remote_copy(
            src_ref=src, dst_ref=dst, send_sem=send, recv_sem=recv,
            device_id=peer, device_id_type=MESH,
        )

    def start(copies):
        for c in copies:
            c.start()
        return copies

    def wait(copies):
        for c in copies:
            c.wait()

    def rows(first, size):
        return pl.ds(pl.multiple_of(first, 8), size)

    loads = start([
        pltpu.make_async_copy(
            x_ref.at[pl.ds(i * tile, tile)], loaded.at[pl.ds(i * tile, tile)], load.at[i]
        )
        for i in range(parts)
    ])
    size = tile * gens

    def add_sum(i):
        loads[i].wait()
        total[...] += jnp.sum(loaded[i * tile : (i + 1) * tile], axis=0)

    def cut(i):
        moved = loaded[i * tile : (i + 1) * tile] - shift[...][None]
        hi, lo = split(moved.reshape(size, loci))
        hi_ref[i * size : (i + 1) * size, :] = hi
        lo_ref[i * size : (i + 1) * size, :] = lo

    def add_upper(i):
        hi, lo = hi_ref[i * size : (i + 1) * size, :], lo_ref[i * size : (i + 1) * size, :]
        upper[...] += tdot16(hi[:, :half], jnp.concatenate([hi, lo], axis=1))
        swapped[...] += tdot16(lo[:, :half], hi[:, half:])

    def add_lower(first, last):
        def body(i, carry):
            at = pl.ds(pl.multiple_of(i * size, size), size)
            hi, lo = hi_ref[at, half:], lo_ref[at, half:]
            lower[...] += tdot16(hi, jnp.concatenate([hi, lo], axis=1))
            return carry

        lax.fori_loop(first, last, body, 0)

    total[...] = jnp.zeros_like(total)
    upper[...] = jnp.zeros_like(upper)
    swapped[...] = jnp.zeros_like(swapped)
    lower[...] = jnp.zeros_like(lower)
    add_sum(0)
    shift[...] = total[...] * (1.0 / tile)
    cut(0)
    for i in range(1, parts):
        add_sum(i)
        cut(i)
        if i < parts - 1:
            add_upper(i - 1)
    tiles = loci // LANES
    own_mean = total[...] * (1.0 / demes)
    for j in range(tiles):
        mu[j * gens : (j + 1) * gens, :] = own_mean[:, j * LANES : (j + 1) * LANES]
    rest = own_mean - shift[...]

    pl.semaphore_wait(barrier, len(peers))
    mrows = mu.shape[0] // nd
    sent = start([
        copy(mu.at[rows((deme + k) % nd * mrows, mrows)], got_mu.at[k - 1],
             send_mu.at[k - 1], recv_mu.at[k - 1], at_deme(k))
        for k in range(1, nd)
    ])
    sent_other = start([copy(mu, mu2, send_other, recv_other, at_core())])
    for i in range(max(parts - 2, 0), parts):
        add_upper(i)
    wait(sent)
    own = rows(deme * mrows, mrows)
    value = mu[own, :]
    for k in range(1, nd):
        value = value + got_mu[k - 1]
    mean[own, :] = value * (1.0 / nd)
    sent_mean = start([
        copy(mean.at[own], mean.at[own], send_mean.at[k - 1], recv_mean.at[k - 1], at_deme(k))
        for k in range(1, nd)
    ] + [
        copy(mean.at[own], mean2.at[own], send_mean2.at[k], recv_mean2.at[k], at_other(k))
        for k in range(nd)
    ])

    def block(i, j):
        rows_, cols = slice(i * LANES, (i + 1) * LANES), slice(j * LANES, (j + 1) * LANES)
        across = slice(j * LANES - half, (j + 1) * LANES - half)
        if i >= half // LANES:
            first = slice(i * LANES - half, (i + 1) * LANES - half)
            again = slice(j * LANES, (j + 1) * LANES)
            value = lower[first, across] + (
                lower[first, again] + lower[across, i * LANES : (i + 1) * LANES].T
            )
        elif j >= half // LANES:
            value = upper[rows_, cols] + (
                upper[rows_, loci + j * LANES : loci + (j + 1) * LANES] + swapped[rows_, across]
            )
        else:
            value = upper[rows_, cols] + (
                upper[rows_, loci + j * LANES : loci + (j + 1) * LANES]
                + upper[cols, loci + i * LANES : loci + (i + 1) * LANES].T
            )
        return value - demes * tdot(rest[:, rows_], rest[:, cols])

    blocks = pairs(loci)

    def put(indices):
        for index in indices:
            acc[index * LANES : (index + 1) * LANES, :] = block(*blocks[index])

    early = [index for index, (i, j) in enumerate(blocks) if i < half // LANES]
    late = [index for index, (i, j) in enumerate(blocks) if i >= half // LANES]
    put(early)
    used = len(blocks) * LANES
    if used < acc.shape[0]:
        acc[used:, :] = jnp.zeros((acc.shape[0] - used, LANES), F32)

    def correct(at0, first, count):
        for index in range(count):
            here = [blocks[b] if b < len(blocks) else (0, 0)
                    for b in (first + index, first + count + index)]
            i = jnp.where(core == 0, here[0][0], here[1][0])
            j = jnp.where(core == 0, here[0][1], here[1][1])
            left = apart[rows(i * 2 * gens, 2 * gens), :]
            right = apart[rows(j * 2 * gens, 2 * gens), :]
            acc[rows(at0 + index * LANES, LANES), :] += demes * tdot(left, right)

    def steps(c, base, unit):
        size1 = unit * nd
        size0 = size1 * nx
        at0 = base * nd * nx * 2 + core * size0
        other0 = base * nd * nx * 2 + (1 - core) * size0
        at1 = at0 + x * size1
        at2 = at1 + deme * unit
        part0 = got_core.at[pl.ds(base * nd * nx, size0)]
        part1 = [got_x.at[k - 1, pl.ds(base * nd, size1)] for k in range(1, nx)]
        part2 = [got_deme.at[k - 1, pl.ds(base, unit)] for k in range(1, nd)]
        sent = start([
            copy(acc.at[rows(other0, size0)], part0, send_core.at[c], recv_core.at[c], at_core())
        ])
        yield
        wait(sent)
        acc[rows(at0, size0), :] += part0[...]
        yield
        correct(at0, base * nd * nx * 2 // LANES, size0 // LANES)
        sent = start([
            copy(acc.at[rows(at0 + (x + k) % nx * size1, size1)], part1[k - 1],
                 send_x.at[c, k - 1], recv_x.at[c, k - 1], at_x(k))
            for k in range(1, nx)
        ])
        yield
        wait(sent)
        value = acc[rows(at1, size1), :]
        for part in part1:
            value = value + part[...]
        acc[rows(at1, size1), :] = value
        sent = start([
            copy(acc.at[rows(at1 + (deme + k) % nd * unit, unit)], part2[k - 1],
                 send_deme.at[c, k - 1], recv_deme.at[c, k - 1], at_deme(k))
            for k in range(1, nd)
        ])
        yield
        wait(sent)
        value = acc[rows(at2, unit), :]
        for part in part2:
            value = value + part[...]
        full[rows(at2, unit), :] = value
        mine = full.at[rows(at2, unit)]
        sent = start([
            copy(mine, mine, send_deme2.at[c, k - 1], recv_deme2.at[c, k - 1], at_deme(k))
            for k in range(1, nd)
        ])
        yield
        wait(sent)
        mine1 = full.at[rows(at1, size1)]
        sent = start([
            copy(mine1, mine1, send_x2.at[c, k - 1], recv_x2.at[c, k - 1], at_x(k))
            for k in range(1, nx)
        ])
        yield
        wait(sent)
        mine0 = full.at[rows(at0, size0)]
        sent = start([copy(mine0, mine0, send_core2.at[c], recv_core2.at[c], at_core())])
        yield
        wait(sent)
        yield

    running, base, ends = [], 0, []
    for c, unit in enumerate(chains(got_deme.shape[1])):
        running.append(steps(c, base, unit))
        base += unit
        ends.append(base * nd * nx * 2 // LANES)
    ahead = [chain for chain, end in zip(running, ends) if end <= len(early)]
    for chain in ahead:
        next(chain)
    add_lower(0, parts)
    put(late)
    for chain in running:
        if chain not in ahead:
            next(chain)
    for chain in running:
        next(chain)
    wait(sent_other)
    wait(sent_mean)
    for j in range(tiles):
        at = slice(j * gens, (j + 1) * gens)
        offset_ref[:, j * LANES : (j + 1) * LANES] = (
            mean[at, :] - shift[:, j * LANES : (j + 1) * LANES]
        )
        apart[j * 2 * gens : j * 2 * gens + gens, :] = mean[at, :] - mu[at, :]
        apart[j * 2 * gens + gens : (j + 1) * 2 * gens, :] = mean2[at, :] - mu2[at, :]
    for _ in range(6):
        for chain in running:
            next(chain)
    out_ref[...] = full[...]


def sum_gram(freqs, packed, nd, nx):
    demes, gens, loci = freqs.shape
    parts = 8 if demes % 8 == 0 else 1
    unit = packed // (2 * nx * nd)
    count = len(chains(unit))
    mshape = (gens * loci // LANES, LANES)
    far = max(nx - 1, 1)
    dma = pltpu.SemaphoreType.DMA
    sems = [dma((count,))] * 2 + [dma((count, far))] * 2 + [dma((count, nd - 1))] * 2
    vmem = pl.BlockSpec(memory_space=pltpu.VMEM)
    return pl.pallas_call(
        functools.partial(gram_kernel, nd, nx),
        in_specs=[pl.BlockSpec(memory_space=pl.ANY)],
        out_specs=[vmem] * 4,
        out_shape=[
            jax.ShapeDtypeStruct((packed, LANES), F32),
            jax.ShapeDtypeStruct((gens, loci), F32),
            pltpu.VMEM((demes * gens, loci), BF16),
            pltpu.VMEM((demes * gens, loci), BF16),
        ],
        scratch_shapes=[
            pltpu.VMEM(freqs.shape, F32),
            pltpu.VMEM((gens, loci), F32),
            pltpu.VMEM((gens, loci), F32),
            pltpu.VMEM((loci // 2, 2 * loci), F32),
            pltpu.VMEM((loci // 2, loci // 2), F32),
            pltpu.VMEM((loci // 2, loci), F32),
            pltpu.VMEM(mshape, F32),
            pltpu.VMEM(mshape, F32),
            pltpu.VMEM((nd - 1, mshape[0] // nd, LANES), F32),
            pltpu.VMEM(mshape, F32),
            pltpu.VMEM(mshape, F32),
            pltpu.VMEM((2 * mshape[0], LANES), F32),
            pltpu.VMEM((packed, LANES), F32),
            pltpu.VMEM((packed // 2, LANES), F32),
            pltpu.VMEM((far, unit * nd, LANES), F32),
            pltpu.VMEM((nd - 1, unit, LANES), F32),
            pltpu.VMEM((packed, LANES), F32),
            dma((parts,)),
        ] + [dma((nd - 1,))] * 4 + [dma((nd,))] * 2 + [dma] * 2 + sems + sems,
        compiler_params=pltpu.CompilerParams(
            collective_id=0, has_side_effects=True, vmem_limit_bytes=32 * 2**20
        ),
        name="sum_gram",
    )(freqs)


def inverse_lower(matrix):
    size = matrix.shape[0]
    shape = (8, size)
    lane = lax.broadcasted_iota(jnp.int32, shape, 1)
    sub = lax.broadcasted_iota(jnp.int32, shape, 0)

    def spread(row):
        return jnp.broadcast_to(row, shape)

    tiles = [matrix[t * 8 : t * 8 + 8, :] for t in range(size // 8)]
    done = []
    for panel in range(len(tiles)):
        first = panel * 8
        inside = (lane >= first) & (lane < first + 8)
        columns = [
            [jnp.broadcast_to(tile[:, first + k : first + k + 1], shape) for k in range(8)]
            for tile in tiles[panel:]
        ]
        entry = {(i, k): spread(columns[0][k][i : i + 1, :]) for k in range(8) for i in range(k, 8)}
        base = jnp.where(inside, jnp.where(lane == first + sub, 1.0, 0.0), tiles[panel])
        scale, rows = [], []
        for k in range(0, 8, 2):
            pivot, beside = entry[k, k], entry[k + 1, k]
            det = pivot * entry[k + 1, k + 1] - beside * beside
            first_scale = lax.rsqrt(pivot)
            scale += [first_scale, (pivot * first_scale) * lax.rsqrt(det)]
            for i in range(k + 1, 8):
                entry[i, k] = entry[i, k] * first_scale
            for i in range(k + 2, 8):
                entry[i, k + 1] = (entry[i, k + 1] - entry[i, k] * entry[k + 1, k]) * scale[k + 1]
            for j in range(k + 2, 8):
                for i in range(j, 8):
                    entry[i, j] = (entry[i, j] - entry[i, k] * entry[j, k]) - (
                        entry[i, k + 1] * entry[j, k + 1]
                    )
        for k in range(8):
            row = spread(base[k : k + 1, :])
            for i in range(k):
                row = row - entry[k, i] * rows[i]
            rows.append(row * scale[k])
        block = rows[0]
        for k in range(1, 8):
            block = jnp.where(sub == k, rows[k], block)
        done.append(jnp.where(lane < first + 8, block, 0.0))
        for t in range(panel + 1, len(tiles)):
            column = columns[t - panel]
            tile = jnp.where(inside, 0.0, tiles[t])
            lower = []
            for k in range(8):
                value = column[k]
                for i in range(k):
                    value = value - lower[i] * entry[k, i]
                lower.append(value * scale[k])
                tile = tile - lower[k] * rows[k]
            tiles[t] = tile
    return jnp.concatenate(done, axis=0)


def split3(a):
    one = a.astype(BF16)
    rest = a - one.astype(F32)
    two = rest.astype(BF16)
    return one, two, (rest - two.astype(F32)).astype(BF16)


def dot16(a, b):
    return jnp.dot(a, b, preferred_element_type=F32)


def basis_kernel(g_ref, start_ref, out_ref, kept, gram1, gram2, gram3):
    loci, rank = start_ref.shape
    on = lax.broadcasted_iota(jnp.int32, (LANES, LANES), 0) == lax.broadcasted_iota(
        jnp.int32, (LANES, LANES), 1
    )
    largest = jnp.zeros((LANES, LANES), F32)
    for index, (i, j) in enumerate(pairs(loci)):
        if i == j:
            block = g_ref[index * LANES : (index + 1) * LANES, :]
            largest = jnp.maximum(largest, jnp.where(on, block, 0.0))
    largest = jnp.max(jnp.max(largest, axis=0, keepdims=True), axis=1, keepdims=True)
    scale = 1.0 / largest
    for index, (i, j) in enumerate(pairs(loci)):
        block = g_ref[index * LANES : (index + 1) * LANES, :] * scale
        rows, cols = slice(i * LANES, (i + 1) * LANES), slice(j * LANES, (j + 1) * LANES)
        for ref, piece in zip((gram1, gram2, gram3), split3(block)):
            ref[rows, cols] = piece
        if i != j:
            for ref, piece in zip((gram1, gram2, gram3), split3(block.T)):
                ref[cols, rows] = piece
    out_ref[...] = start_ref[...]

    def step(_, carry):
        q1, q2, q3 = split3(out_ref[...])
        both = jnp.concatenate([q1, q2], axis=1)
        large, small = dot16(gram1[...], both), dot16(gram2[...], both)
        rest = dot16(gram1[...], q3) + dot16(gram3[...], q1)
        z = large[:, :rank] + (large[:, rank:] + (small[:, :rank] + (small[:, rank:] + rest)))
        z1, z2, z3 = split3(z)
        both = jnp.concatenate([z1, z2], axis=1)
        square = tdot16(both, both)
        rest = tdot16(z1, z3)
        rest = rest + rest.T + square[rank:, rank:]
        small = square[:rank, :rank] + (square[:rank, rank:] + (square[rank:, :rank] + rest))
        w1, w2, w3 = split3(inverse_lower(small))
        right = jnp.concatenate(
            [jnp.concatenate([w1, w1], axis=1), jnp.concatenate([w2, w2], axis=1)], axis=0
        )
        contract = (((1,), (1,)), ((), ()))
        large = lax.dot_general(both, right, contract, preferred_element_type=F32)
        rest = lax.dot_general(
            jnp.concatenate([z3, z1], axis=1), jnp.concatenate([w1, w3], axis=1), contract,
            preferred_element_type=F32,
        )
        out_ref[...] = large[:, :rank] + (large[:, rank:] + rest)
        return carry

    lax.fori_loop(0, ITERS, step, 0)
    kept[...] = out_ref[...]


def find_basis(gram, start):
    loci, rank = start.shape
    return pl.pallas_call(
        basis_kernel,
        in_specs=[pl.BlockSpec(memory_space=pltpu.VMEM)] * 2,
        out_specs=[pl.BlockSpec(memory_space=pltpu.VMEM)] * 2,
        out_shape=[jax.ShapeDtypeStruct(start.shape, F32), pltpu.VMEM(start.shape, F32)],
        scratch_shapes=[
            pltpu.VMEM((loci, loci), BF16),
            pltpu.VMEM((loci, loci), BF16),
            pltpu.VMEM((loci, loci), BF16),
        ],
        compiler_params=pltpu.CompilerParams(vmem_limit_bytes=16 * 2**20),
        name="find_basis",
    )(gram, start)


def core_kernel(hi_ref, lo_ref, offset_ref, factor_ref, out_ref):
    demes, gens, rank = out_ref.shape
    fhi, flo = split(factor_ref[...])
    pieces = jnp.concatenate([fhi, flo], axis=1)
    ohi, olo = split(offset_ref[...])
    both = dot16(ohi, pieces)
    offset = both[:, :rank] + (both[:, rank:] + dot16(olo, fhi))
    part = 8 if demes % 8 == 0 else demes
    size = part * gens
    first = pl.program_id(0) * demes * gens
    for at in range(0, demes, part):
        here = pl.ds(pl.multiple_of(first + at * gens, size), size)
        both = dot16(hi_ref[here, :], pieces)
        value = both[:, :rank] + (both[:, rank:] + dot16(lo_ref[here, :], fhi))
        out_ref[at : at + part] = value.reshape(part, gens, rank) - offset[None]


def find_core(hi, lo, offset, factor):
    gens, rank = offset.shape[0], factor.shape[1]
    demes = hi.shape[0] // gens
    tile = 32 if demes % 32 == 0 else demes
    vmem = pl.BlockSpec(memory_space=pltpu.VMEM)
    hi, lo = (pltpu.with_memory_space_constraint(a, pltpu.VMEM) for a in (hi, lo))
    return pl.pallas_call(
        core_kernel,
        grid=(demes // tile,),
        in_specs=[vmem] * 4,
        out_specs=pl.BlockSpec((tile, gens, rank), lambda i: (i, 0, 0)),
        out_shape=jax.ShapeDtypeStruct((demes, gens, rank), F32),
        compiler_params=pltpu.CompilerParams(vmem_limit_bytes=16 * 2**20),
        name="find_core",
    )(hi, lo, offset, factor)


def solution(mesh):
    nd, ng = mesh.shape["deme"], mesh.shape["gen"]
    nx = ng // 2

    def local(freqs, start_basis):
        demes, gens, loci = freqs.shape
        unit = 8 * nd * ng
        packed = -(-len(pairs(loci)) * LANES // unit) * unit
        gram, offset, hi, lo = sum_gram(freqs, packed, nd, nx)
        factor, near = find_basis(gram, start_basis)
        return find_core(hi, lo, offset, near), factor

    in_specs = (P("deme", "gen", None), P())
    out_specs = (P("deme", "gen", None), P())
    return jax.shard_map(local, mesh=mesh, in_specs=in_specs, out_specs=out_specs, check_vma=False)
```

```python
import functools

import jax
import jax.numpy as jnp
from jax import lax
from jax.experimental import pallas as pl
from jax.experimental.pallas import tpu as pltpu
from jax.sharding import PartitionSpec as P

ITERS = 4
MESH = pl.DeviceIdType.MESH
HIGHEST = lax.Precision.HIGHEST
F32 = jnp.float32
BF16 = jnp.bfloat16
LANES = 128


def dot(a, b):
    return jnp.dot(a, b, precision=HIGHEST, preferred_element_type=F32)


def tdot(a, b):
    return lax.dot_general(
        a, b, (((0,), (0,)), ((), ())), precision=HIGHEST, preferred_element_type=F32
    )


def tdot16(a, b):
    return lax.dot_general(a, b, (((0,), (0,)), ((), ())), preferred_element_type=F32)


def split(a):
    hi = a.astype(BF16)
    return hi, (a - hi.astype(F32)).astype(BF16)


def pairs(loci):
    tiles = loci // LANES
    return [(i, j) for i in range(tiles) for j in range(i, tiles)]


def chains(unit):
    first = unit // 16 * 8
    return [first, unit - first] if first else [unit]


def gram_kernel(
    nd, nx, x_ref, out_ref, mean_ref, kept,
    shift, total, upper, lower, mu, mean, got_mu, acc, got_core, got_x, got_deme, full,
    load, send_mu, recv_mu, send_mu2, recv_mu2,
    send_core, recv_core, send_x, recv_x, send_deme, recv_deme,
    send_core2, recv_core2, send_x2, recv_x2, send_deme2, recv_deme2,
):
    demes, gens, loci = x_ref.shape
    half = loci // 2
    parts = load.shape[0]
    tile = demes // parts
    deme = lax.axis_index("deme")
    gen = lax.axis_index("gen")
    x, core = gen // 2, gen % 2

    def at_core():
        return (deme, x * 2 + (1 - core))

    def at_x(k):
        return (deme, ((x + k) % nx) * 2 + core)

    def at_deme(k):
        return ((deme + k) % nd, gen)

    peers = [at_core()] + [at_x(k) for k in range(1, nx)] + [at_deme(k) for k in range(1, nd)]
    barrier = pltpu.get_barrier_semaphore()
    for peer in peers:
        pl.semaphore_signal(barrier, inc=1, device_id=peer, device_id_type=MESH)

    def copy(src, dst, send, recv, peer):
        return pltpu.make_async_remote_copy(
            src_ref=src, dst_ref=dst, send_sem=send, recv_sem=recv,
            device_id=peer, device_id_type=MESH,
        )

    def start(copies):
        for c in copies:
            c.start()
        return copies

    def wait(copies):
        for c in copies:
            c.wait()

    def rows(first, size):
        return pl.ds(pl.multiple_of(first, 8), size)

    loads = start([
        pltpu.make_async_copy(
            x_ref.at[pl.ds(i * tile, tile)], kept.at[pl.ds(i * tile, tile)], load.at[i]
        )
        for i in range(parts)
    ])

    def add_sum(i):
        loads[i].wait()
        total[...] += jnp.sum(kept[i * tile : (i + 1) * tile], axis=0)

    def add_gram(i):
        moved = kept[pl.ds(i * tile, tile)] - shift[...][None]
        hi, lo = split(moved.reshape(tile * gens, loci))
        upper[...] += tdot16(jnp.concatenate([hi, lo], axis=1), hi[:, :half])
        lower[...] += tdot16(jnp.concatenate([hi[:, half:], lo], axis=1), hi[:, half:])

    def grams(first, last):
        def body(i, carry):
            add_gram(i)
            return carry

        lax.fori_loop(first, last, body, 0)

    total[...] = jnp.zeros_like(total)
    upper[...] = jnp.zeros_like(upper)
    lower[...] = jnp.zeros_like(lower)
    add_sum(0)
    shift[...] = total[...] * (1.0 / tile)
    early = parts // 4
    for i in range(1, parts // 2):
        add_sum(i)
    grams(0, early)
    for i in range(max(parts // 2, 1), parts):
        add_sum(i)
    tiles = loci // LANES
    own_mean = total[...] * (1.0 / demes)
    for j in range(tiles):
        mu[j * gens : (j + 1) * gens, :] = own_mean[:, j * LANES : (j + 1) * LANES]
    rest = own_mean - shift[...]

    pl.semaphore_wait(barrier, len(peers))
    mrows = mu.shape[0] // nd
    sent = start([
        copy(mu.at[rows((deme + k) % nd * mrows, mrows)], got_mu.at[k - 1],
             send_mu.at[k - 1], recv_mu.at[k - 1], at_deme(k))
        for k in range(1, nd)
    ])
    middle = (early + parts + 1) // 2
    grams(early, middle)
    wait(sent)
    own = rows(deme * mrows, mrows)
    value = mu[own, :]
    for k in range(1, nd):
        value = value + got_mu[k - 1]
    mean[own, :] = value * (1.0 / nd)
    sent = start([
        copy(mean.at[own], mean.at[own], send_mu2.at[k - 1], recv_mu2.at[k - 1], at_deme(k))
        for k in range(1, nd)
    ])
    grams(middle, parts)
    wait(sent)
    mean_ref[...] = mean[...]

    def piece(first, j):
        if j < half // LANES:
            return upper[first : first + LANES, j * LANES : (j + 1) * LANES]
        return lower[first - half : first - half + LANES, j * LANES - half : (j + 1) * LANES - half]

    apart = [
        mean[j * gens : (j + 1) * gens, :] - mu[j * gens : (j + 1) * gens, :] for j in range(tiles)
    ]
    moved = [rest[:, j * LANES : (j + 1) * LANES] for j in range(tiles)]
    left = [jnp.concatenate([a, b], axis=0) for a, b in zip(apart, moved)]
    right = [jnp.concatenate([a, -b], axis=0) for a, b in zip(apart, moved)]
    for index, (i, j) in enumerate(pairs(loci)):
        block = piece(j * LANES, i) + piece(loci + j * LANES, i)
        block = block.T + piece(loci + i * LANES, j)
        acc[index * LANES : (index + 1) * LANES, :] = block + demes * tdot(left[i], right[j])
    used = len(pairs(loci)) * LANES
    if used < acc.shape[0]:
        acc[used:, :] = jnp.zeros((acc.shape[0] - used, LANES), F32)

    def steps(c, base, unit):
        size1 = unit * nd
        size0 = size1 * nx
        at0 = base * nd * nx * 2 + core * size0
        other0 = base * nd * nx * 2 + (1 - core) * size0
        at1 = at0 + x * size1
        at2 = at1 + deme * unit
        part0 = got_core.at[pl.ds(base * nd * nx, size0)]
        part1 = [got_x.at[k - 1, pl.ds(base * nd, size1)] for k in range(1, nx)]
        part2 = [got_deme.at[k - 1, pl.ds(base, unit)] for k in range(1, nd)]
        sent = start([
            copy(acc.at[rows(other0, size0)], part0, send_core.at[c], recv_core.at[c], at_core())
        ])
        yield
        wait(sent)
        acc[rows(at0, size0), :] += part0[...]
        sent = start([
            copy(acc.at[rows(at0 + (x + k) % nx * size1, size1)], part1[k - 1],
                 send_x.at[c, k - 1], recv_x.at[c, k - 1], at_x(k))
            for k in range(1, nx)
        ])
        yield
        wait(sent)
        value = acc[rows(at1, size1), :]
        for part in part1:
            value = value + part[...]
        acc[rows(at1, size1), :] = value
        sent = start([
            copy(acc.at[rows(at1 + (deme + k) % nd * unit, unit)], part2[k - 1],
                 send_deme.at[c, k - 1], recv_deme.at[c, k - 1], at_deme(k))
            for k in range(1, nd)
        ])
        yield
        wait(sent)
        value = acc[rows(at2, unit), :]
        for part in part2:
            value = value + part[...]
        full[rows(at2, unit), :] = value
        mine = full.at[rows(at2, unit)]
        sent = start([
            copy(mine, mine, send_deme2.at[c, k - 1], recv_deme2.at[c, k - 1], at_deme(k))
            for k in range(1, nd)
        ])
        yield
        wait(sent)
        mine1 = full.at[rows(at1, size1)]
        sent = start([
            copy(mine1, mine1, send_x2.at[c, k - 1], recv_x2.at[c, k - 1], at_x(k))
            for k in range(1, nx)
        ])
        yield
        wait(sent)
        mine0 = full.at[rows(at0, size0)]
        sent = start([copy(mine0, mine0, send_core2.at[c], recv_core2.at[c], at_core())])
        yield
        wait(sent)
        yield

    running, base = [], 0
    for c, unit in enumerate(chains(got_deme.shape[1])):
        running.append(steps(c, base, unit))
        base += unit
    for _ in range(7):
        for chain in running:
            next(chain)
    out_ref[...] = full[...]


def sum_gram(freqs, packed, nd, nx):
    demes, gens, loci = freqs.shape
    parts = 8 if demes % 8 == 0 else 1
    unit = packed // (2 * nx * nd)
    count = len(chains(unit))
    mshape = (gens * loci // LANES, LANES)
    far = max(nx - 1, 1)
    dma = pltpu.SemaphoreType.DMA
    sems = [dma((count,))] * 2 + [dma((count, far))] * 2 + [dma((count, nd - 1))] * 2
    vmem = pl.BlockSpec(memory_space=pltpu.VMEM)
    return pl.pallas_call(
        functools.partial(gram_kernel, nd, nx),
        in_specs=[pl.BlockSpec(memory_space=pl.ANY)],
        out_specs=[vmem, vmem, vmem],
        out_shape=[
            jax.ShapeDtypeStruct((packed, LANES), F32),
            jax.ShapeDtypeStruct(mshape, F32),
            pltpu.VMEM(freqs.shape, F32),
        ],
        scratch_shapes=[
            pltpu.VMEM((gens, loci), F32),
            pltpu.VMEM((gens, loci), F32),
            pltpu.VMEM((2 * loci, loci // 2), F32),
            pltpu.VMEM((loci + loci // 2, loci // 2), F32),
            pltpu.VMEM(mshape, F32),
            pltpu.VMEM(mshape, F32),
            pltpu.VMEM((nd - 1, mshape[0] // nd, LANES), F32),
            pltpu.VMEM((packed, LANES), F32),
            pltpu.VMEM((packed // 2, LANES), F32),
            pltpu.VMEM((far, unit * nd, LANES), F32),
            pltpu.VMEM((nd - 1, unit, LANES), F32),
            pltpu.VMEM((packed, LANES), F32),
            dma((parts,)),
        ] + [dma((nd - 1,))] * 4 + sems + sems,
        compiler_params=pltpu.CompilerParams(
            collective_id=0, has_side_effects=True, vmem_limit_bytes=30 * 2**20
        ),
        name="sum_gram",
    )(freqs)


def inverse_lower(matrix):
    size = matrix.shape[0]
    shape = (8, size)
    lane = lax.broadcasted_iota(jnp.int32, shape, 1)
    sub = lax.broadcasted_iota(jnp.int32, shape, 0)

    def spread(row):
        return jnp.broadcast_to(row, shape)

    tiles = [matrix[t * 8 : t * 8 + 8, :] for t in range(size // 8)]
    done, blocks, group = [], [], 4
    for panel in range(len(tiles)):
        first = panel * 8
        end = min((panel // group + 1) * group, len(tiles))
        inside = (lane >= first) & (lane < first + 8)
        columns = [
            [jnp.broadcast_to(tile[:, first + k : first + k + 1], shape) for k in range(8)]
            for tile in tiles[panel:end]
        ]
        entry = {(i, k): spread(columns[0][k][i : i + 1, :]) for k in range(8) for i in range(k, 8)}
        base = jnp.where(inside, jnp.where(lane == first + sub, 1.0, 0.0), tiles[panel])
        scale, rows = [], []
        for k in range(8):
            scale.append(lax.rsqrt(entry[k, k]))
            for i in range(k + 1, 8):
                entry[i, k] = entry[i, k] * scale[k]
            for j in range(k + 1, 8):
                for i in range(j, 8):
                    entry[i, j] = entry[i, j] - entry[i, k] * entry[j, k]
        for k in range(8):
            row = spread(base[k : k + 1, :])
            for i in range(k):
                row = row - entry[k, i] * rows[i]
            rows.append(row * scale[k])
        block = rows[0]
        for k in range(1, 8):
            block = jnp.where(sub == k, rows[k], block)
        done.append(jnp.where(lane < first + 8, block, 0.0))
        for t in range(panel + 1, end):
            column = columns[t - panel]
            tile = jnp.where(inside, 0.0, tiles[t])
            lower = []
            for k in range(8):
                value = column[k]
                for i in range(k):
                    value = value - lower[i] * entry[k, i]
                lower.append(value * scale[k])
                tile = tile - lower[k] * rows[k]
            tiles[t] = tile
        blocks.append(block)
        if panel + 1 == end and end < len(tiles):
            later = lane >= end * 8
            left = [jnp.where(later, b, 0.0) for b in blocks[-group:]]
            right = [jnp.where(later, b, d) for b, d in zip(blocks[-group:], done[-group:])]
            change = tdot(jnp.concatenate(left, axis=0), jnp.concatenate(right, axis=0))
            inside = (lane >= (end - group) * 8) & (lane < end * 8)
            for t in range(end, len(tiles)):
                tiles[t] = jnp.where(inside, 0.0, tiles[t]) - change[t * 8 : t * 8 + 8, :]
    return jnp.concatenate(done, axis=0)


def split3(a):
    one = a.astype(BF16)
    rest = a - one.astype(F32)
    two = rest.astype(BF16)
    return one, two, (rest - two.astype(F32)).astype(BF16)


def dot16(a, b):
    return jnp.dot(a, b, preferred_element_type=F32)


def basis_kernel(scale, g_ref, start_ref, out_ref, kept, gram1, gram2, gram3):
    loci, rank = start_ref.shape
    for index, (i, j) in enumerate(pairs(loci)):
        block = g_ref[index * LANES : (index + 1) * LANES, :] * scale
        rows, cols = slice(i * LANES, (i + 1) * LANES), slice(j * LANES, (j + 1) * LANES)
        for ref, piece in zip((gram1, gram2, gram3), split3(block)):
            ref[rows, cols] = piece
        if i != j:
            for ref, piece in zip((gram1, gram2, gram3), split3(block.T)):
                ref[cols, rows] = piece
    out_ref[...] = start_ref[...]

    def step(_, carry):
        q1, q2, q3 = split3(out_ref[...])
        both = jnp.concatenate([q1, q2], axis=1)
        large, small = dot16(gram1[...], both), dot16(gram2[...], both)
        rest = dot16(gram1[...], q3) + dot16(gram3[...], q1)
        z = large[:, :rank] + (large[:, rank:] + (small[:, :rank] + (small[:, rank:] + rest)))
        z1, z2, z3 = split3(z)
        both = jnp.concatenate([z1, z2], axis=1)
        square = tdot16(both, both)
        rest = tdot16(z1, z3)
        rest = rest + rest.T + square[rank:, rank:]
        small = square[:rank, :rank] + (square[:rank, rank:] + (square[rank:, :rank] + rest))
        w1, w2, w3 = split3(inverse_lower(small))
        right = jnp.concatenate(
            [jnp.concatenate([w1, w1], axis=1), jnp.concatenate([w2, w2], axis=1)], axis=0
        )
        contract = (((1,), (1,)), ((), ()))
        large = lax.dot_general(both, right, contract, preferred_element_type=F32)
        rest = lax.dot_general(
            jnp.concatenate([z3, z1], axis=1), jnp.concatenate([w1, w3], axis=1), contract,
            preferred_element_type=F32,
        )
        out_ref[...] = large[:, :rank] + (large[:, rank:] + rest)
        return carry

    lax.fori_loop(0, ITERS, step, 0)
    kept[...] = out_ref[...]


def find_basis(gram, start, scale):
    loci, rank = start.shape
    return pl.pallas_call(
        functools.partial(basis_kernel, scale),
        in_specs=[pl.BlockSpec(memory_space=pltpu.VMEM)] * 2,
        out_specs=[pl.BlockSpec(memory_space=pltpu.VMEM)] * 2,
        out_shape=[jax.ShapeDtypeStruct(start.shape, F32), pltpu.VMEM(start.shape, F32)],
        scratch_shapes=[
            pltpu.VMEM((loci, loci), BF16),
            pltpu.VMEM((loci, loci), BF16),
            pltpu.VMEM((loci, loci), BF16),
        ],
        compiler_params=pltpu.CompilerParams(vmem_limit_bytes=30 * 2**20),
        name="find_basis",
    )(gram, start)


def core_kernel(x_ref, mean_ref, factor_ref, out_ref):
    demes, gens, rank = out_ref.shape
    loci = x_ref.shape[2]
    mean = jnp.concatenate(
        [mean_ref[j * gens : (j + 1) * gens, :] for j in range(loci // LANES)], axis=1
    )
    fhi, flo = split(factor_ref[...])
    pieces = jnp.concatenate([fhi, flo], axis=1)
    part = demes
    first = pl.program_id(0) * demes
    for at in range(0, demes, part):
        hi, lo = split((x_ref[pl.ds(first + at, part)] - mean[None]).reshape(part * gens, loci))
        both = dot16(hi, pieces)
        value = both[:, :rank] + (both[:, rank:] + dot16(lo, fhi))
        out_ref[at : at + part] = value.reshape(part, gens, rank)


def find_core(freqs, mean, factor):
    demes, gens, loci = freqs.shape
    rank = factor.shape[1]
    tile = 32 if demes % 32 == 0 else demes
    vmem = pl.BlockSpec(memory_space=pltpu.VMEM)
    return pl.pallas_call(
        core_kernel,
        grid=(demes // tile,),
        in_specs=[vmem, vmem, vmem],
        out_specs=pl.BlockSpec((tile, gens, rank), lambda i: (i, 0, 0)),
        out_shape=jax.ShapeDtypeStruct((demes, gens, rank), F32),
        compiler_params=pltpu.CompilerParams(vmem_limit_bytes=30 * 2**20),
        name="find_core",
    )(pltpu.with_memory_space_constraint(freqs, pltpu.VMEM), mean, factor)


def solution(mesh):
    nd, ng = mesh.shape["deme"], mesh.shape["gen"]
    nx = ng // 2

    def local(freqs, start_basis):
        demes, gens, loci = freqs.shape
        unit = 8 * nd * ng
        packed = -(-len(pairs(loci)) * LANES // unit) * unit
        gram, mean, kept = sum_gram(freqs, packed, nd, nx)
        scale = 1.0 / (demes * nd * gens * ng)
        factor, near = find_basis(gram, start_basis, scale)
        return find_core(kept, mean, near), factor

    in_specs = (P("deme", "gen", None), P())
    out_specs = (P("deme", "gen", None), P())
    return jax.shard_map(local, mesh=mesh, in_specs=in_specs, out_specs=out_specs, check_vma=False)
```

```python
import functools

import jax
import jax.numpy as jnp
from jax import lax
from jax.experimental import pallas as pl
from jax.experimental.pallas import tpu as pltpu
from jax.sharding import PartitionSpec as P

ITERS = 4
MESH = pl.DeviceIdType.MESH
HIGHEST = lax.Precision.HIGHEST
F32 = jnp.float32
BF16 = jnp.bfloat16
LANES = 128


def dot(a, b):
    return jnp.dot(a, b, precision=HIGHEST, preferred_element_type=F32)


def tdot(a, b):
    return lax.dot_general(
        a, b, (((0,), (0,)), ((), ())), precision=HIGHEST, preferred_element_type=F32
    )


def tdot16(a, b):
    return lax.dot_general(a, b, (((0,), (0,)), ((), ())), preferred_element_type=F32)


def split(a):
    hi = a.astype(BF16)
    return hi, (a - hi.astype(F32)).astype(BF16)


def pairs(loci):
    tiles = loci // LANES
    return [(i, j) for i in range(tiles) for j in range(i, tiles)]


def chains(unit):
    first = unit // 16 * 8
    return [first, unit - first] if first else [unit]


def gram_kernel(
    nd, nx, x_ref, out_ref, mean_ref, kept,
    shift, total, upper, lower, mu, mean, got_mu, acc, got_core, got_x, got_deme, full,
    load, send_mu, recv_mu, send_mu2, recv_mu2,
    send_core, recv_core, send_x, recv_x, send_deme, recv_deme,
    send_core2, recv_core2, send_x2, recv_x2, send_deme2, recv_deme2,
):
    demes, gens, loci = x_ref.shape
    half = loci // 2
    parts = load.shape[0]
    tile = demes // parts
    deme = lax.axis_index("deme")
    gen = lax.axis_index("gen")
    x, core = gen // 2, gen % 2

    def at_core():
        return (deme, x * 2 + (1 - core))

    def at_x(k):
        return (deme, ((x + k) % nx) * 2 + core)

    def at_deme(k):
        return ((deme + k) % nd, gen)

    peers = [at_core()] + [at_x(k) for k in range(1, nx)] + [at_deme(k) for k in range(1, nd)]
    barrier = pltpu.get_barrier_semaphore()
    for peer in peers:
        pl.semaphore_signal(barrier, inc=1, device_id=peer, device_id_type=MESH)

    def copy(src, dst, send, recv, peer):
        return pltpu.make_async_remote_copy(
            src_ref=src, dst_ref=dst, send_sem=send, recv_sem=recv,
            device_id=peer, device_id_type=MESH,
        )

    def start(copies):
        for c in copies:
            c.start()
        return copies

    def wait(copies):
        for c in copies:
            c.wait()

    def rows(first, size):
        return pl.ds(pl.multiple_of(first, 8), size)

    loads = start([
        pltpu.make_async_copy(
            x_ref.at[pl.ds(i * tile, tile)], kept.at[pl.ds(i * tile, tile)], load.at[i]
        )
        for i in range(parts)
    ])

    def add_sum(i):
        loads[i].wait()
        total[...] += jnp.sum(kept[i * tile : (i + 1) * tile], axis=0)

    def add_gram(i):
        moved = kept[pl.ds(i * tile, tile)] - shift[...][None]
        hi, lo = split(moved.reshape(tile * gens, loci))
        upper[...] += tdot16(jnp.concatenate([hi, lo], axis=1), hi[:, :half])
        lower[...] += tdot16(jnp.concatenate([hi[:, half:], lo], axis=1), hi[:, half:])

    def grams(first, last):
        def body(i, carry):
            add_gram(i)
            return carry

        lax.fori_loop(first, last, body, 0)

    total[...] = jnp.zeros_like(total)
    upper[...] = jnp.zeros_like(upper)
    lower[...] = jnp.zeros_like(lower)
    add_sum(0)
    shift[...] = total[...] * (1.0 / tile)
    early = parts // 4
    for i in range(1, parts // 2):
        add_sum(i)
    grams(0, early)
    for i in range(max(parts // 2, 1), parts):
        add_sum(i)
    tiles = loci // LANES
    own_mean = total[...] * (1.0 / demes)
    for j in range(tiles):
        mu[j * gens : (j + 1) * gens, :] = own_mean[:, j * LANES : (j + 1) * LANES]
    rest = own_mean - shift[...]

    pl.semaphore_wait(barrier, len(peers))
    mrows = mu.shape[0] // nd
    sent = start([
        copy(mu.at[rows((deme + k) % nd * mrows, mrows)], got_mu.at[k - 1],
             send_mu.at[k - 1], recv_mu.at[k - 1], at_deme(k))
        for k in range(1, nd)
    ])
    middle = (early + parts + 1) // 2
    grams(early, middle)
    wait(sent)
    own = rows(deme * mrows, mrows)
    value = mu[own, :]
    for k in range(1, nd):
        value = value + got_mu[k - 1]
    mean[own, :] = value * (1.0 / nd)
    sent = start([
        copy(mean.at[own], mean.at[own], send_mu2.at[k - 1], recv_mu2.at[k - 1], at_deme(k))
        for k in range(1, nd)
    ])
    grams(middle, parts)
    wait(sent)
    mean_ref[...] = mean[...]

    def piece(first, j):
        if j < half // LANES:
            return upper[first : first + LANES, j * LANES : (j + 1) * LANES]
        return lower[first - half : first - half + LANES, j * LANES - half : (j + 1) * LANES - half]

    apart = [
        mean[j * gens : (j + 1) * gens, :] - mu[j * gens : (j + 1) * gens, :] for j in range(tiles)
    ]
    moved = [rest[:, j * LANES : (j + 1) * LANES] for j in range(tiles)]
    left = [jnp.concatenate([a, b], axis=0) for a, b in zip(apart, moved)]
    right = [jnp.concatenate([a, -b], axis=0) for a, b in zip(apart, moved)]
    for index, (i, j) in enumerate(pairs(loci)):
        block = piece(j * LANES, i) + piece(loci + j * LANES, i)
        block = block.T + piece(loci + i * LANES, j)
        acc[index * LANES : (index + 1) * LANES, :] = block + demes * tdot(left[i], right[j])
    used = len(pairs(loci)) * LANES
    if used < acc.shape[0]:
        acc[used:, :] = jnp.zeros((acc.shape[0] - used, LANES), F32)

    def steps(c, base, unit):
        size1 = unit * nd
        size0 = size1 * nx
        at0 = base * nd * nx * 2 + core * size0
        other0 = base * nd * nx * 2 + (1 - core) * size0
        at1 = at0 + x * size1
        at2 = at1 + deme * unit
        part0 = got_core.at[pl.ds(base * nd * nx, size0)]
        part1 = [got_x.at[k - 1, pl.ds(base * nd, size1)] for k in range(1, nx)]
        part2 = [got_deme.at[k - 1, pl.ds(base, unit)] for k in range(1, nd)]
        sent = start([
            copy(acc.at[rows(other0, size0)], part0, send_core.at[c], recv_core.at[c], at_core())
        ])
        yield
        wait(sent)
        acc[rows(at0, size0), :] += part0[...]
        sent = start([
            copy(acc.at[rows(at0 + (x + k) % nx * size1, size1)], part1[k - 1],
                 send_x.at[c, k - 1], recv_x.at[c, k - 1], at_x(k))
            for k in range(1, nx)
        ])
        yield
        wait(sent)
        value = acc[rows(at1, size1), :]
        for part in part1:
            value = value + part[...]
        acc[rows(at1, size1), :] = value
        sent = start([
            copy(acc.at[rows(at1 + (deme + k) % nd * unit, unit)], part2[k - 1],
                 send_deme.at[c, k - 1], recv_deme.at[c, k - 1], at_deme(k))
            for k in range(1, nd)
        ])
        yield
        wait(sent)
        value = acc[rows(at2, unit), :]
        for part in part2:
            value = value + part[...]
        full[rows(at2, unit), :] = value
        mine = full.at[rows(at2, unit)]
        sent = start([
            copy(mine, mine, send_deme2.at[c, k - 1], recv_deme2.at[c, k - 1], at_deme(k))
            for k in range(1, nd)
        ])
        yield
        wait(sent)
        mine1 = full.at[rows(at1, size1)]
        sent = start([
            copy(mine1, mine1, send_x2.at[c, k - 1], recv_x2.at[c, k - 1], at_x(k))
            for k in range(1, nx)
        ])
        yield
        wait(sent)
        mine0 = full.at[rows(at0, size0)]
        sent = start([copy(mine0, mine0, send_core2.at[c], recv_core2.at[c], at_core())])
        yield
        wait(sent)
        yield

    running, base = [], 0
    for c, unit in enumerate(chains(got_deme.shape[1])):
        running.append(steps(c, base, unit))
        base += unit
    for _ in range(7):
        for chain in running:
            next(chain)
    out_ref[...] = full[...]


def sum_gram(freqs, packed, nd, nx):
    demes, gens, loci = freqs.shape
    parts = 8 if demes % 8 == 0 else 1
    unit = packed // (2 * nx * nd)
    count = len(chains(unit))
    mshape = (gens * loci // LANES, LANES)
    far = max(nx - 1, 1)
    dma = pltpu.SemaphoreType.DMA
    sems = [dma((count,))] * 2 + [dma((count, far))] * 2 + [dma((count, nd - 1))] * 2
    vmem = pl.BlockSpec(memory_space=pltpu.VMEM)
    return pl.pallas_call(
        functools.partial(gram_kernel, nd, nx),
        in_specs=[pl.BlockSpec(memory_space=pl.ANY)],
        out_specs=[vmem, vmem, vmem],
        out_shape=[
            jax.ShapeDtypeStruct((packed, LANES), F32),
            jax.ShapeDtypeStruct(mshape, F32),
            pltpu.VMEM(freqs.shape, F32),
        ],
        scratch_shapes=[
            pltpu.VMEM((gens, loci), F32),
            pltpu.VMEM((gens, loci), F32),
            pltpu.VMEM((2 * loci, loci // 2), F32),
            pltpu.VMEM((loci + loci // 2, loci // 2), F32),
            pltpu.VMEM(mshape, F32),
            pltpu.VMEM(mshape, F32),
            pltpu.VMEM((nd - 1, mshape[0] // nd, LANES), F32),
            pltpu.VMEM((packed, LANES), F32),
            pltpu.VMEM((packed // 2, LANES), F32),
            pltpu.VMEM((far, unit * nd, LANES), F32),
            pltpu.VMEM((nd - 1, unit, LANES), F32),
            pltpu.VMEM((packed, LANES), F32),
            dma((parts,)),
        ] + [dma((nd - 1,))] * 4 + sems + sems,
        compiler_params=pltpu.CompilerParams(
            collective_id=0, has_side_effects=True, vmem_limit_bytes=30 * 2**20
        ),
        name="sum_gram",
    )(freqs)


def inverse_lower(matrix):
    size = matrix.shape[0]
    shape = (8, size)
    lane = lax.broadcasted_iota(jnp.int32, shape, 1)
    sub = lax.broadcasted_iota(jnp.int32, shape, 0)

    def spread(row):
        return jnp.broadcast_to(row, shape)

    tiles = [matrix[t * 8 : t * 8 + 8, :] for t in range(size // 8)]
    done, blocks, group = [], [], 4
    for panel in range(len(tiles)):
        first = panel * 8
        end = min((panel // group + 1) * group, len(tiles))
        inside = (lane >= first) & (lane < first + 8)
        columns = [
            [jnp.broadcast_to(tile[:, first + k : first + k + 1], shape) for k in range(8)]
            for tile in tiles[panel:end]
        ]
        entry = {(i, k): spread(columns[0][k][i : i + 1, :]) for k in range(8) for i in range(k, 8)}
        base = jnp.where(inside, jnp.where(lane == first + sub, 1.0, 0.0), tiles[panel])
        scale, rows = [], []
        for k in range(0, 8, 2):
            pivot, beside = entry[k, k], entry[k + 1, k]
            det = pivot * entry[k + 1, k + 1] - beside * beside
            first_scale = lax.rsqrt(pivot)
            scale += [first_scale, (pivot * first_scale) * lax.rsqrt(det)]
            for i in range(k + 1, 8):
                entry[i, k] = entry[i, k] * first_scale
            for i in range(k + 2, 8):
                entry[i, k + 1] = (entry[i, k + 1] - entry[i, k] * entry[k + 1, k]) * scale[k + 1]
            for j in range(k + 2, 8):
                for i in range(j, 8):
                    entry[i, j] = (entry[i, j] - entry[i, k] * entry[j, k]) - (
                        entry[i, k + 1] * entry[j, k + 1]
                    )
        for k in range(8):
            row = spread(base[k : k + 1, :])
            for i in range(k):
                row = row - entry[k, i] * rows[i]
            rows.append(row * scale[k])
        block = rows[0]
        for k in range(1, 8):
            block = jnp.where(sub == k, rows[k], block)
        done.append(jnp.where(lane < first + 8, block, 0.0))
        for t in range(panel + 1, end):
            column = columns[t - panel]
            tile = jnp.where(inside, 0.0, tiles[t])
            lower = []
            for k in range(8):
                value = column[k]
                for i in range(k):
                    value = value - lower[i] * entry[k, i]
                lower.append(value * scale[k])
                tile = tile - lower[k] * rows[k]
            tiles[t] = tile
        blocks.append(block)
        if panel + 1 == end and end < len(tiles):
            later = lane >= end * 8
            left = [jnp.where(later, b, 0.0) for b in blocks[-group:]]
            right = [jnp.where(later, b, d) for b, d in zip(blocks[-group:], done[-group:])]
            change = tdot(jnp.concatenate(left, axis=0), jnp.concatenate(right, axis=0))
            inside = (lane >= (end - group) * 8) & (lane < end * 8)
            for t in range(end, len(tiles)):
                tiles[t] = jnp.where(inside, 0.0, tiles[t]) - change[t * 8 : t * 8 + 8, :]
    return jnp.concatenate(done, axis=0)


def split3(a):
    one = a.astype(BF16)
    rest = a - one.astype(F32)
    two = rest.astype(BF16)
    return one, two, (rest - two.astype(F32)).astype(BF16)


def dot16(a, b):
    return jnp.dot(a, b, preferred_element_type=F32)


def basis_kernel(g_ref, start_ref, out_ref, kept, gram):
    loci, rank = start_ref.shape
    on = lax.broadcasted_iota(jnp.int32, (LANES, LANES), 0) == lax.broadcasted_iota(
        jnp.int32, (LANES, LANES), 1
    )
    largest = jnp.zeros((LANES, LANES), F32)
    for index, (i, j) in enumerate(pairs(loci)):
        if i == j:
            block = g_ref[index * LANES : (index + 1) * LANES, :]
            largest = jnp.maximum(largest, jnp.where(on, block, 0.0))
    largest = jnp.max(jnp.max(largest, axis=0, keepdims=True), axis=1, keepdims=True)
    scale = 1.0 / largest
    for index, (i, j) in enumerate(pairs(loci)):
        block = g_ref[index * LANES : (index + 1) * LANES, :] * scale
        rows, cols = slice(i * LANES, (i + 1) * LANES), slice(j * LANES, (j + 1) * LANES)
        for at, piece in zip((loci, 2 * loci, 0), split3(block)):
            gram[rows, at + j * LANES : at + (j + 1) * LANES] = piece
        if i != j:
            for at, piece in zip((loci, 2 * loci, 0), split3(block.T)):
                gram[cols, at + i * LANES : at + (i + 1) * LANES] = piece
    out_ref[...] = start_ref[...]

    def step(_, carry):
        q1, q2, q3 = split3(out_ref[...])
        both = jnp.concatenate([q1, q2], axis=1)
        large = dot16(gram[:, loci:], jnp.concatenate([both, both], axis=0))
        rest = dot16(gram[:, : 2 * loci], jnp.concatenate([q1, q3], axis=0))
        z = large[:, :rank] + (large[:, rank:] + rest)
        z1, z2, z3 = split3(z)
        both = jnp.concatenate([z1, z2], axis=1)
        square = tdot16(both, both)
        rest = tdot16(z1, z3)
        rest = rest + rest.T + square[rank:, rank:]
        small = square[:rank, :rank] + (square[:rank, rank:] + (square[rank:, :rank] + rest))
        w1, w2, w3 = split3(inverse_lower(small))
        none = jnp.zeros_like(w1)
        right = jnp.concatenate(
            [
                jnp.concatenate([w1, w1, w1, w3], axis=1),
                jnp.concatenate([w2, w2, none, none], axis=1),
            ],
            axis=0,
        )
        large = lax.dot_general(
            jnp.concatenate([z1, z2, z3, z1], axis=1), right, (((1,), (1,)), ((), ())),
            preferred_element_type=F32,
        )
        out_ref[...] = large[:, :rank] + large[:, rank:]
        return carry

    lax.fori_loop(0, ITERS, step, 0)
    kept[...] = out_ref[...]


def find_basis(gram, start):
    loci, rank = start.shape
    return pl.pallas_call(
        basis_kernel,
        in_specs=[pl.BlockSpec(memory_space=pltpu.VMEM)] * 2,
        out_specs=[pl.BlockSpec(memory_space=pltpu.VMEM)] * 2,
        out_shape=[jax.ShapeDtypeStruct(start.shape, F32), pltpu.VMEM(start.shape, F32)],
        scratch_shapes=[
            pltpu.VMEM((loci, 3 * loci), BF16),
        ],
        compiler_params=pltpu.CompilerParams(vmem_limit_bytes=30 * 2**20),
        name="find_basis",
    )(gram, start)


def core_kernel(x_ref, mean_ref, factor_ref, out_ref):
    demes, gens, rank = out_ref.shape
    loci = x_ref.shape[2]
    mean = jnp.concatenate(
        [mean_ref[j * gens : (j + 1) * gens, :] for j in range(loci // LANES)], axis=1
    )
    fhi, flo = split(factor_ref[...])
    pieces = jnp.concatenate([fhi, flo], axis=1)
    pieces = jnp.concatenate([pieces, pieces], axis=0)
    part = demes
    first = pl.program_id(0) * demes
    for at in range(0, demes, part):
        hi, lo = split((x_ref[pl.ds(first + at, part)] - mean[None]).reshape(part * gens, loci))
        both = dot16(jnp.concatenate([hi, lo], axis=1), pieces)
        value = both[:, :rank] + both[:, rank:]
        out_ref[at : at + part] = value.reshape(part, gens, rank)


def find_core(freqs, mean, factor):
    demes, gens, loci = freqs.shape
    rank = factor.shape[1]
    tile = 32 if demes % 32 == 0 else demes
    vmem = pl.BlockSpec(memory_space=pltpu.VMEM)
    return pl.pallas_call(
        core_kernel,
        grid=(demes // tile,),
        in_specs=[vmem, vmem, vmem],
        out_specs=pl.BlockSpec((tile, gens, rank), lambda i: (i, 0, 0)),
        out_shape=jax.ShapeDtypeStruct((demes, gens, rank), F32),
        compiler_params=pltpu.CompilerParams(vmem_limit_bytes=30 * 2**20),
        name="find_core",
    )(pltpu.with_memory_space_constraint(freqs, pltpu.VMEM), mean, factor)


def solution(mesh):
    nd, ng = mesh.shape["deme"], mesh.shape["gen"]
    nx = ng // 2

    def local(freqs, start_basis):
        demes, gens, loci = freqs.shape
        unit = 8 * nd * ng
        packed = -(-len(pairs(loci)) * LANES // unit) * unit
        gram, mean, kept = sum_gram(freqs, packed, nd, nx)
        factor, near = find_basis(gram, start_basis)
        return find_core(kept, mean, near), factor

    in_specs = (P("deme", "gen", None), P())
    out_specs = (P("deme", "gen", None), P())
    return jax.shard_map(local, mesh=mesh, in_specs=in_specs, out_specs=out_specs, check_vma=False)
```
